32 devices in a mesh: head: 2 (over y), replica: 16 (over z, x, core).
Axes of the slice: x: 2, y: 2, z: 4, core: 2. Of those that a mesh axis runs over, the one named last changes fastest.
Arguments:
- queries: bfloat16 [16, 256, 512], P('replica', None, 'head'), may hold values from -1.5 to 1.5
- keys: bfloat16 [16, 256, 512], P('replica', None, 'head'), may hold values from -1.5 to 1.5
- values: bfloat16 [16, 256, 512], P('replica', None, 'head'), may hold values from -6 to 6
- out_weight: bfloat16 [4096, 512], P('replica', 'head'), may hold values from -0.25 to 0.25
- cotangent: bfloat16 [16, 256, 4096], P('replica'), may hold values from -6 to 6
- on_time: int32 [16], P('replica'), may hold values from 0 to 1, as said below
Outputs:
- layer_out: bfloat16 [16, 256, 4096], P('replica')
- value_grad: bfloat16 [16, 256, 512], P('replica', None, 'head')
- weight_grad: float32 [4096, 512], P('replica', 'head')
The draws below stay inside these ranges and needn't reach their ends.
Inputs may be any that keep to these rules, and one draw needn't show every extreme that they name: `on_time`: at least one replica is on time.
All inputs are finite; a program needn't handle non-finite values.
Results may differ from the reference program's by a relative error of at most 0.022.
Values may be sent and summed in bfloat16 or wider, within the bound.
A program may use at most 64 MiB of HBM per device.

```python
import jax
import jax.numpy as jnp

D = 4096
DH = 256
DV = 256
TOK = 256
HEADS = 2
HQ = 512
HD = 512
REPLICAS = 16


def draw_on_time(key, part):
    key = jax.random.fold_in(key, 7)
    first, second = jax.random.split(key)
    ticket = jax.random.randint(first, (REPLICAS,), 0, 4)
    forced = jax.random.randint(second, (), 0, REPLICAS)
    chosen = jnp.arange(REPLICAS) == forced
    return jnp.where((ticket > 0) | chosen, 1, 0).astype(jnp.int32)


def level_of(key, extent, shards, least, largest):
    def one(dim, blocks):
        steps = jax.random.uniform(jax.random.fold_in(jax.random.fold_in(key, 6), dim), (blocks,), jnp.float32, least / len(shards), largest / len(shards))
        return jnp.repeat(jnp.exp(steps), extent[dim] // blocks).reshape((-1,) + (1,) * (len(extent) - dim - 1))

    factor_of = one(*shards[0])
    for cut in shards[1:]:
        factor_of = factor_of * one(*cut)
    return factor_of


def bell_draw(stream_key, dims, spread, reach, cuts=(), held_as=jnp.bfloat16):
    values = spread * jax.random.normal(stream_key, dims, jnp.float32)
    if cuts:
        values = values * level_of(stream_key, dims, cuts, -0.22, 0.18)
    return jnp.clip(values, -reach, reach).astype(held_as)


def setup_inputs(seed: int = 0) -> dict:
    key_of = jax.random.split(jax.random.key(seed), 7)
    return {
        "queries": bell_draw(key_of[0], (REPLICAS, TOK, HQ), 0.25, 1.5, ((0, 16), (2, 2))),
        "keys": bell_draw(key_of[1], (REPLICAS, TOK, HQ), 0.25, 1.5, ((0, 16), (2, 2))),
        "values": bell_draw(key_of[2], (REPLICAS, TOK, HD), 1.0, 6.0, ((0, 16), (2, 2))),
        "out_weight": bell_draw(key_of[3], (D, HD), HD ** -0.5, 0.25, ((0, 16), (1, 2))),
        "cotangent": bell_draw(key_of[4], (REPLICAS, TOK, D), 1.0, 6.0, ((0, 16),)),
        "on_time": draw_on_time(jax.random.fold_in(key_of[6], 71), 0),
    }


def reference(queries, keys, values, out_weight, cotangent, on_time):
    shape_qk = (REPLICAS, TOK, HEADS, DH)
    shape_v = (REPLICAS, TOK, HEADS, DV)
    qf = queries.astype(jnp.float32).reshape(shape_qk)
    kf = keys.astype(jnp.float32).reshape(shape_qk)
    vf = values.astype(jnp.float32).reshape(shape_v)
    position = jnp.arange(TOK)
    offset = (position[:, None] - position[None, :]).astype(jnp.float32)
    heads = jnp.arange(HEADS).astype(jnp.float32)
    gamma = 1.0 - 2.0 ** (-5.0 - heads)
    decay = jnp.where(offset[None] >= 0.0, jnp.exp(jnp.maximum(offset[None], 0.0) * jnp.log(gamma)[:, None, None]), 0.0)
    scores = jnp.einsum("rnhd,rmhd->rhnm", qf, kf) * decay[None]
    denom = jnp.maximum(jnp.sum(jnp.abs(scores), axis=-1, keepdims=True), 1.0)
    weights = (scores / denom).astype(jnp.bfloat16)
    wf = weights.astype(jnp.float32)
    mixed = jnp.einsum("rhnm,rmhd->rnhd", wf, vf).astype(jnp.bfloat16).reshape(REPLICAS * TOK, HD)
    total = jnp.zeros((REPLICAS * TOK, D), jnp.float32)
    for head in range(HEADS):
        piece = mixed[:, head * DV:(head + 1) * DV]
        rows = out_weight[:, head * DV:(head + 1) * DV]
        term = jax.lax.dot_general(piece, rows, (((1,), (1,)), ((), ())), preferred_element_type=jnp.float32)
        total = total + term.astype(jnp.bfloat16).astype(jnp.float32)
    layer_out = total.astype(jnp.bfloat16).reshape(REPLICAS, TOK, D)
    flat_cot = cotangent.reshape(REPLICAS * TOK, D)
    mixed_grad = jnp.dot(flat_cot, out_weight, preferred_element_type=jnp.float32).astype(jnp.bfloat16)
    dof = mixed_grad.astype(jnp.float32).reshape(shape_v)
    value_grad = jnp.einsum("rhnm,rnhd->rmhd", wf, dof).astype(jnp.bfloat16).reshape(REPLICAS, TOK, HD)
    accepted = jnp.sum(on_time).astype(jnp.int32)
    keep = jnp.repeat(on_time.astype(jnp.bfloat16), TOK)[:, None]
    masked = mixed * keep
    summed = jax.lax.dot_general(flat_cot, masked, (((0,), (0,)), ((), ())), preferred_element_type=jnp.float32)
    weight_grad = summed / accepted.astype(jnp.float32)
    return layer_out, value_grad, weight_grad
```

```python
import functools
import math

import jax
import jax.numpy as jnp
from jax import lax
from jax.experimental import pallas as pl
from jax.experimental.pallas import tpu as pltpu
from jax.sharding import PartitionSpec as P

MESH = pl.DeviceIdType.MESH
FLAG_ROWS = 16
F32 = jnp.float32
BF16 = jnp.bfloat16


def dot(a, b, dims):
    return lax.dot_general(a, b, ((dims[:1], dims[1:]), ((), ())), preferred_element_type=F32)


def each(count, body):
    if count <= 4:
        for i in range(count):
            body(i)
    else:
        lax.fori_loop(0, count, lambda i, c: (body(i), c)[1], 0)


def when(cond, body):
    if isinstance(cond, bool):
        if cond:
            body()
    else:
        pl.when(cond)(body)


def kernel(
    heads, replicas,
    q_hbm, k_hbm, v_hbm, w_hbm, cot_hbm, on_ref,
    layer_hbm, value_grad_ref, weight_grad_ref,
    q, k, v, cot, layer, w_all, mixed_all, mixed_grad, part, weights_ref,
    core_out, core_in, x_out, x_in, z_out, up_in, down_in,
    load_sem, layer_sem,
    w_recv, up_send, down_send, x_send, head_send, core_send,
    mixed_send, mixed_recv,
    core_out_sem, core_in_sem, x_out_sem, x_in_sem, z_out_sem, up_sem, down_sem,
):
    depth = replicas // 4
    rows = w_hbm.shape[0]
    group = 4 * rows
    tokens = q.shape[0]
    head = lax.axis_index("head")
    me = lax.axis_index("replica")
    z, x, c = me // 4, (me // 2) % 2, me % 2

    def rep(zz, xx, cc):
        return zz * 4 + xx * 2 + cc

    sibling = (head, rep(z, x, 1 - c))
    across = (head, rep(z, 1 - x, c))
    above = (head, rep(z + 1, x, c))
    below = (head, rep(z - 1, x, c))

    def peer(j):
        return lax.rem(head + 1 + j, heads)

    barrier = pltpu.get_barrier_semaphore()

    def greet(device):
        pl.semaphore_signal(barrier, inc=1, device_id=device, device_id_type=MESH)

    greet(sibling)
    greet(across)
    each(heads - 1, lambda j: greet((peer(j), me)))
    pl.when(z > 0)(lambda: greet(below))
    pl.when(z < depth - 1)(lambda: greet(above))

    loads = [
        pltpu.make_async_copy(src, dst, load_sem.at[i])
        for i, (src, dst) in enumerate(
            ((q_hbm.at[0], q), (k_hbm.at[0], k), (v_hbm.at[0], v), (cot_hbm.at[0], cot),
             (w_hbm, w_all.at[head, pl.ds(pl.multiple_of(me * rows, rows), rows)]))
        )
    ]
    for load in loads:
        load.start()
    pl.semaphore_wait(
        barrier, 1 + heads + jnp.where(z > 0, 1, 0) + jnp.where(z < depth - 1, 1, 0)
    )

    def block(hh, rr):
        return w_all.at[hh, pl.ds(pl.multiple_of(rr * rows, rows), rows)]

    def w_copy(hh, rr, sem, device, src=None):
        return pltpu.make_async_remote_copy(
            src_ref=block(hh, rr) if src is None else src,
            dst_ref=block(hh, rr),
            send_sem=sem,
            recv_sem=w_recv.at[hh, rr],
            device_id=device,
            device_id_type=MESH,
        )

    def w_wait(hh, rr):
        w_copy(hh, rr, core_send.at[hh, rr], sibling).wait_recv()

    def to_above(rr, src=None):
        return w_copy(head, rr, up_send.at[rr], above, src)

    def to_below(rr, src=None):
        return w_copy(head, rr, down_send.at[rr], below, src)

    def to_across(rr, src=None):
        return w_copy(head, rr, x_send.at[rr], across, src)

    def to_peer(j, rr, src=None):
        return w_copy(head, rr, head_send.at[j, rr], (peer(j), me), src)

    def to_core(hh, rr, src=None):
        return w_copy(hh, rr, core_send.at[hh, rr], sibling, src)

    def spread(rr, src=None):
        each(heads - 1, lambda j: to_peer(j, rr, src).start())
        to_core(head, rr, src).start()

    pl.when(z < depth - 1)(lambda: to_above(me, w_hbm).start())
    pl.when(z > 0)(lambda: to_below(me, w_hbm).start())
    to_across(me, w_hbm).start()
    spread(me, w_hbm)

    def around(d, body):
        if isinstance(d, int) and d == 0:
            body(z, None)
        else:
            pl.when(z - d >= 0)(lambda: body(z - d, True))
            pl.when(z + d < depth)(lambda: body(z + d, False))

    def gather_z(d):
        def body(zz, went_up):
            rr = rep(zz, x, c)
            w_wait(head, rr)
            if went_up:
                pl.when(z < depth - 1)(lambda: to_above(rr).start())
            else:
                pl.when(z > 0)(lambda: to_below(rr).start())
            to_across(rr).start()
            spread(rr)

        around(d, body)

    def gather_x(d):
        def body(zz, _):
            rr = rep(zz, 1 - x, c)
            w_wait(head, rr)
            spread(rr)

        around(d, body)

    def gather_heads(d):
        def body(zz, _):
            def from_peer(j):
                for xx in (x, 1 - x):
                    rr = rep(zz, xx, c)
                    w_wait(peer(j), rr)
                    to_core(peer(j), rr).start()

            each(heads - 1, from_peer)

        around(d, body)

    def core_wait(hh, zz):
        for xx in (0, 1):
            w_wait(hh, rep(zz, xx, 1 - c))

    for load in loads[:3]:
        load.wait()
    row = lax.broadcasted_iota(jnp.int32, (tokens, tokens), 0)
    col = lax.broadcasted_iota(jnp.int32, (tokens, tokens), 1)
    offset = (row - col).astype(F32)
    log_gamma = jnp.float32(math.log(1.0 - 2.0 ** -5.0))
    for i in range(1, heads):
        log_gamma = jnp.where(head == i, jnp.float32(math.log(1.0 - 2.0 ** (-5.0 - i))), log_gamma)
    decay = jnp.where(offset >= 0.0, jnp.exp(jnp.maximum(offset, 0.0) * log_gamma), 0.0)
    scores = dot(q[...], k[...], (1, 1)) * decay
    denom = jnp.maximum(jnp.sum(jnp.abs(scores), axis=-1, keepdims=True), 1.0)
    weights_ref[...] = (scores / denom).astype(BF16)
    mixed_all[head] = dot(weights_ref[...], v[...], (1, 0)).astype(BF16)

    def mixed_copy(j):
        return pltpu.make_async_remote_copy(
            src_ref=mixed_all.at[head],
            dst_ref=mixed_all.at[head],
            send_sem=mixed_send.at[j],
            recv_sem=mixed_recv.at[head],
            device_id=(peer(j), me),
            device_id_type=MESH,
        )

    def mixed_wait(j):
        pltpu.make_async_remote_copy(
            src_ref=mixed_all.at[peer(j)],
            dst_ref=mixed_all.at[peer(j)],
            send_sem=mixed_send.at[j],
            recv_sem=mixed_recv.at[peer(j)],
            device_id=(peer(j), me),
            device_id_type=MESH,
        ).wait_recv()

    each(heads - 1, lambda j: mixed_copy(j).start())

    on = on_ref[0].astype(F32)
    flags = jnp.full((FLAG_ROWS, part.shape[1]), 1.0, F32) * on
    body_rows = pl.ds(0, rows)
    flag_rows = pl.ds(rows, FLAG_ROWS)

    def order(i):
        if isinstance(i, int):
            return i // 2 if i % 2 == 0 else depth - 1 - i // 2
        return jnp.where(i % 2 == 0, i // 2, depth - 1 - i // 2)

    def own_part(rr):
        return part[pl.ds(pl.multiple_of(rr * rows, rows), rows)]

    def core_copy(slot):
        return pltpu.make_async_remote_copy(
            core_out.at[slot], core_in.at[slot], core_out_sem.at[slot], core_in_sem.at[slot],
            device_id=sibling, device_id_type=MESH,
        )

    def x_copy(zz):
        return pltpu.make_async_remote_copy(
            x_out.at[zz], x_in.at[zz], x_out_sem.at[zz], x_in_sem.at[zz],
            device_id=across, device_id_type=MESH,
        )

    def up_copy(zz):
        return pltpu.make_async_remote_copy(
            z_out.at[zz], up_in.at[zz], z_out_sem.at[zz], up_sem.at[zz],
            device_id=above, device_id_type=MESH,
        )

    def down_copy(zz):
        return pltpu.make_async_remote_copy(
            z_out.at[zz], down_in.at[zz], z_out_sem.at[zz], down_sem.at[zz],
            device_id=below, device_id_type=MESH,
        )

    loads[3].wait()
    masked = mixed_all[head] * on.astype(BF16)

    def sum_start(i):
        zz = order(i)
        at = pl.multiple_of(zz * group, group)
        part[pl.ds(at, group)] = dot(cot[:, pl.ds(at, group)], masked, (0, 0))
        for xx in (1 - x, x):
            slot = zz * 2 + xx
            core_out[slot, body_rows] = own_part(rep(zz, xx, 1 - c)).astype(BF16)
            core_out[slot, flag_rows] = flags.astype(BF16)
            core_copy(slot).start()

    def sum_x(i):
        zz = order(i)
        slot = zz * 2 + 1 - x
        core_copy(slot).wait_recv()
        x_out[zz, body_rows] = (
            own_part(rep(zz, 1 - x, c)) + core_in[slot, body_rows].astype(F32)
        ).astype(BF16)
        x_out[zz, flag_rows] = (flags + core_in[slot, flag_rows].astype(F32)).astype(BF16)
        x_copy(zz).start()

    def local_sum(zz):
        slot = zz * 2 + x
        core_copy(slot).wait_recv()
        x_copy(zz).wait_recv()
        main = (
            own_part(rep(zz, x, c))
            + core_in[slot, body_rows].astype(F32)
            + x_in[zz, body_rows].astype(F32)
        )
        flag = (
            flags + core_in[slot, flag_rows].astype(F32) + x_in[zz, flag_rows].astype(F32)
        )
        return main, flag

    def put(dst, zz, main, flag):
        dst[zz, body_rows] = main.astype(BF16)
        dst[zz, flag_rows] = flag.astype(BF16)

    def plus(pair, src, zz):
        return (
            pair[0] + src[zz, body_rows].astype(F32),
            pair[1] + src[zz, flag_rows].astype(F32),
        )

    def sum_z(i):
        zz = jnp.where(z < depth // 2, depth - 1 - order(i), order(i))

        @pl.when(zz > z)
        def _():
            pair = local_sum(zz)

            @pl.when(z == 0)
            def _():
                put(z_out, zz, *pair)

            @pl.when(z > 0)
            def _():
                up_copy(zz).wait_recv()
                put(z_out, zz, *plus(pair, up_in, zz))

            up_copy(zz).start()

        @pl.when(zz < z)
        def _():
            pair = local_sum(zz)

            @pl.when(z == depth - 1)
            def _():
                put(z_out, zz, *pair)

            @pl.when(z < depth - 1)
            def _():
                down_copy(zz).wait_recv()
                put(z_out, zz, *plus(pair, down_in, zz))

            down_copy(zz).start()

    def sum_end():
        main, flag = local_sum(z)
        part[pl.ds(0, rows)] = main
        part[pl.ds(rows, FLAG_ROWS)] = flag

        def add(src, copy):
            copy(z).wait_recv()
            part[pl.ds(0, rows)] += src[z, body_rows].astype(F32)
            part[pl.ds(rows, FLAG_ROWS)] += src[z, flag_rows].astype(F32)

        pl.when(z > 0)(lambda: add(up_in, up_copy))
        pl.when(z < depth - 1)(lambda: add(down_in, down_copy))
        weight_grad_ref[...] = part[pl.ds(0, rows)] / part[pl.ds(rows, 1)]

    def columns(zz):
        return pl.ds(pl.multiple_of(zz * group, group), group)

    def grad_group(d):
        def body(zz, _):
            core_wait(head, zz)
            mixed_grad[...] += dot(cot[:, columns(zz)], w_all[head, columns(zz)], (1, 0))

        around(d, body)

    def layer_copy(zz):
        return pltpu.make_async_copy(
            layer.at[:, columns(zz)], layer_hbm.at[0, :, columns(zz)], layer_sem.at[zz]
        )

    def term(hh, zz):
        return dot(mixed_all[hh], w_all[hh, columns(zz)], (1, 1)).astype(BF16).astype(F32)

    def layer_group(d):
        def body(zz, _):
            each(heads - 1, lambda j: core_wait(peer(j), zz))
            total = term(0, zz)
            if heads <= 4:
                for i in range(1, heads):
                    total = total + term(i, zz)
            else:
                total = lax.fori_loop(1, heads, lambda i, t: t + term(i, zz), total)
            layer[:, columns(zz)] = total.astype(BF16)
            layer_copy(zz).start()

        around(d, body)

    each(depth, sum_start)
    gather_z(1)
    gather_x(0)
    for i in range(depth):
        sum_x(i)
        if i + 2 < depth:
            gather_z(i + 2)
        if i + 1 < depth:
            gather_x(i + 1)
    mixed_grad[...] = jnp.zeros_like(mixed_grad)
    loads[4].wait()
    for i in range(depth):
        gather_heads(i)
        sum_z(i)
        grad_group(i)
        if i == 0:
            each(heads - 1, mixed_wait)
        if i > 0:
            layer_group(i - 1)
    value_grad_ref[0] = dot(
        weights_ref[...], mixed_grad[...].astype(BF16), (0, 0)
    ).astype(BF16)
    layer_group(depth - 1)
    sum_end()

    each(depth, lambda i: layer_copy(i).wait())
    each(heads - 1, lambda j: mixed_copy(j).wait_send())

    def drain(zz):
        for xx in (0, 1):
            rr = rep(zz, xx, c)
            each(heads - 1, lambda j: to_peer(j, rr).wait_send())
            each(heads, lambda hh: to_core(hh, rr).wait_send())
            core_copy(zz * 2 + xx).wait_send()
        rr = rep(zz, x, c)
        to_across(rr).wait_send()
        x_copy(zz).wait_send()
        pl.when((zz <= z) & (z < depth - 1))(lambda: to_above(rr).wait_send())
        pl.when((zz >= z) & (z > 0))(lambda: to_below(rr).wait_send())
        pl.when(zz > z)(lambda: up_copy(zz).wait_send())
        pl.when(zz < z)(lambda: down_copy(zz).wait_send())

    each(depth, drain)


def local(heads, replicas, queries, keys, values, out_weight, cotangent, on_time):
    _, tokens, features = queries.shape
    value_features = values.shape[2]
    rows = out_weight.shape[0]
    model = cotangent.shape[2]
    depth = replicas // 4
    summed = (rows + FLAG_ROWS, value_features)
    any_spec = pl.BlockSpec(memory_space=pl.ANY)
    vmem = pl.BlockSpec(memory_space=pltpu.VMEM)
    dma = pltpu.SemaphoreType.DMA
    return pl.pallas_call(
        functools.partial(kernel, heads, replicas),
        out_shape=(
            jax.ShapeDtypeStruct(cotangent.shape, BF16),
            jax.ShapeDtypeStruct(values.shape, BF16),
            jax.ShapeDtypeStruct(out_weight.shape, F32),
        ),
        in_specs=[any_spec] * 5 + [pl.BlockSpec(memory_space=pltpu.SMEM)],
        out_specs=(any_spec, vmem, vmem),
        scratch_shapes=[
            pltpu.VMEM((tokens, features), BF16),
            pltpu.VMEM((tokens, features), BF16),
            pltpu.VMEM((tokens, value_features), BF16),
            pltpu.VMEM((tokens, model), BF16),
            pltpu.VMEM((tokens, model), BF16),
            pltpu.VMEM((heads, model, value_features), BF16),
            pltpu.VMEM((heads, tokens, value_features), BF16),
            pltpu.VMEM((tokens, value_features), F32),
            pltpu.VMEM((model, value_features), F32),
            pltpu.VMEM((tokens, tokens), BF16),
            pltpu.VMEM((depth * 2,) + summed, BF16),
            pltpu.VMEM((depth * 2,) + summed, BF16),
            pltpu.VMEM((depth,) + summed, BF16),
            pltpu.VMEM((depth,) + summed, BF16),
            pltpu.VMEM((depth,) + summed, BF16),
            pltpu.VMEM((depth,) + summed, BF16),
            pltpu.VMEM((depth,) + summed, BF16),
            dma((5,)),
            dma((depth,)),
            dma((heads, replicas)),
            dma((replicas,)),
            dma((replicas,)),
            dma((replicas,)),
            dma((heads, replicas)),
            dma((heads, replicas)),
            dma((heads,)),
            dma((heads,)),
            dma((depth * 2,)),
            dma((depth * 2,)),
            dma((depth,)),
            dma((depth,)),
            dma((depth,)),
            dma((depth,)),
            dma((depth,)),
        ],
        compiler_params=pltpu.CompilerParams(
            collective_id=0, has_side_effects=True, vmem_limit_bytes=48 * 1024 * 1024
        ),
    )(queries, keys, values, out_weight, cotangent, on_time)


def solution(mesh):
    return jax.shard_map(
        functools.partial(local, mesh.shape["head"], mesh.shape["replica"]),
        mesh=mesh,
        in_specs=(
            P("replica", None, "head"),
            P("replica", None, "head"),
            P("replica", None, "head"),
            P("replica", "head"),
            P("replica", None, None),
            P("replica"),
        ),
        out_specs=(P("replica", None, None), P("replica", None, "head"), P("replica", "head")),
        check_vma=False,
    )
```

```python
import functools
import math

import jax
import jax.numpy as jnp
from jax import lax
from jax.experimental import pallas as pl
from jax.experimental.pallas import tpu as pltpu
from jax.sharding import PartitionSpec as P

MESH = pl.DeviceIdType.MESH
FLAG_ROWS = 16
F32 = jnp.float32
BF16 = jnp.bfloat16


def dot(a, b, dims):
    return lax.dot_general(a, b, ((dims[:1], dims[1:]), ((), ())), preferred_element_type=F32)


def each(count, body):
    if count <= 4:
        for i in range(count):
            body(i)
    else:
        lax.fori_loop(0, count, lambda i, c: (body(i), c)[1], 0)


def when(cond, body):
    if isinstance(cond, bool):
        if cond:
            body()
    else:
        pl.when(cond)(body)


def kernel(
    heads, replicas,
    q_hbm, k_hbm, v_hbm, w_hbm, cot_hbm, on_ref,
    layer_hbm, value_grad_ref, weight_grad_ref,
    q, k, v, cot, layer, w_all, mixed_all, mixed_grad, part, weights_ref,
    core_out, core_in, x_out, x_in, z_out, up_in, down_in,
    load_sem, layer_sem,
    w_recv, up_send, down_send, x_send, head_send, core_send,
    mixed_send, mixed_recv,
    core_out_sem, core_in_sem, x_out_sem, x_in_sem, z_out_sem, up_sem, down_sem,
):
    depth = replicas // 4
    rows = w_hbm.shape[0]
    group = 4 * rows
    tokens = q.shape[0]
    head = lax.axis_index("head")
    me = lax.axis_index("replica")
    z, x, c = me // 4, (me // 2) % 2, me % 2

    def rep(zz, xx, cc):
        return zz * 4 + xx * 2 + cc

    sibling = (head, rep(z, x, 1 - c))
    across = (head, rep(z, 1 - x, c))
    above = (head, rep(z + 1, x, c))
    below = (head, rep(z - 1, x, c))

    def peer(j):
        return lax.rem(head + 1 + j, heads)

    barrier = pltpu.get_barrier_semaphore()

    def greet(device):
        pl.semaphore_signal(barrier, inc=1, device_id=device, device_id_type=MESH)

    greet(sibling)
    greet(across)
    each(heads - 1, lambda j: greet((peer(j), me)))
    pl.when(z > 0)(lambda: greet(below))
    pl.when(z < depth - 1)(lambda: greet(above))

    loads = [
        pltpu.make_async_copy(src, dst, load_sem.at[i])
        for i, (src, dst) in enumerate(
            ((q_hbm.at[0], q), (k_hbm.at[0], k), (v_hbm.at[0], v), (cot_hbm.at[0], cot),
             (w_hbm, w_all.at[head, pl.ds(pl.multiple_of(me * rows, rows), rows)]))
        )
    ]
    for load in loads:
        load.start()
    pl.semaphore_wait(
        barrier, 1 + heads + jnp.where(z > 0, 1, 0) + jnp.where(z < depth - 1, 1, 0)
    )

    def block(hh, rr):
        return w_all.at[hh, pl.ds(pl.multiple_of(rr * rows, rows), rows)]

    def w_copy(hh, rr, sem, device, src=None):
        return pltpu.make_async_remote_copy(
            src_ref=block(hh, rr) if src is None else src,
            dst_ref=block(hh, rr),
            send_sem=sem,
            recv_sem=w_recv.at[hh, rr],
            device_id=device,
            device_id_type=MESH,
        )

    def w_wait(hh, rr):
        w_copy(hh, rr, core_send.at[hh, rr], sibling).wait_recv()

    def to_above(rr, src=None):
        return w_copy(head, rr, up_send.at[rr], above, src)

    def to_below(rr, src=None):
        return w_copy(head, rr, down_send.at[rr], below, src)

    def to_across(rr, src=None):
        return w_copy(head, rr, x_send.at[rr], across, src)

    def to_peer(j, rr, src=None):
        return w_copy(head, rr, head_send.at[j, rr], (peer(j), me), src)

    def to_core(hh, rr, src=None):
        return w_copy(hh, rr, core_send.at[hh, rr], sibling, src)

    def spread(rr, src=None):
        each(heads - 1, lambda j: to_peer(j, rr, src).start())
        to_core(head, rr, src).start()

    pl.when(z < depth - 1)(lambda: to_above(me, w_hbm).start())
    pl.when(z > 0)(lambda: to_below(me, w_hbm).start())
    to_across(me, w_hbm).start()
    spread(me, w_hbm)

    def around(d, body):
        if isinstance(d, int) and d == 0:
            body(z, None)
        else:
            pl.when(z - d >= 0)(lambda: body(z - d, True))
            pl.when(z + d < depth)(lambda: body(z + d, False))

    def gather_z(d):
        def body(zz, went_up):
            rr = rep(zz, x, c)
            w_wait(head, rr)
            if went_up:
                pl.when(z < depth - 1)(lambda: to_above(rr).start())
            else:
                pl.when(z > 0)(lambda: to_below(rr).start())
            spread(rr)

        around(d, body)

    def send_x(d):
        around(d, lambda zz, _: to_across(rep(zz, x, c)).start())

    def gather_x(d):
        def body(zz, _):
            rr = rep(zz, 1 - x, c)
            w_wait(head, rr)
            spread(rr)

        around(d, body)

    def gather_heads(d):
        def body(zz, _):
            def from_peer(j):
                for xx in (x, 1 - x):
                    rr = rep(zz, xx, c)
                    w_wait(peer(j), rr)
                    to_core(peer(j), rr).start()

            each(heads - 1, from_peer)

        around(d, body)

    def core_wait(hh, zz):
        for xx in (0, 1):
            w_wait(hh, rep(zz, xx, 1 - c))

    for load in loads[:3]:
        load.wait()
    row = lax.broadcasted_iota(jnp.int32, (tokens, tokens), 0)
    col = lax.broadcasted_iota(jnp.int32, (tokens, tokens), 1)
    offset = (row - col).astype(F32)
    log_gamma = jnp.float32(math.log(1.0 - 2.0 ** -5.0))
    for i in range(1, heads):
        log_gamma = jnp.where(head == i, jnp.float32(math.log(1.0 - 2.0 ** (-5.0 - i))), log_gamma)
    decay = jnp.where(offset >= 0.0, jnp.exp(jnp.maximum(offset, 0.0) * log_gamma), 0.0)
    scores = dot(q[...], k[...], (1, 1)) * decay
    denom = jnp.maximum(jnp.sum(jnp.abs(scores), axis=-1, keepdims=True), 1.0)
    weights_ref[...] = (scores / denom).astype(BF16)
    mixed_all[head] = dot(weights_ref[...], v[...], (1, 0)).astype(BF16)

    def mixed_copy(j):
        return pltpu.make_async_remote_copy(
            src_ref=mixed_all.at[head],
            dst_ref=mixed_all.at[head],
            send_sem=mixed_send.at[j],
            recv_sem=mixed_recv.at[head],
            device_id=(peer(j), me),
            device_id_type=MESH,
        )

    def mixed_wait(j):
        pltpu.make_async_remote_copy(
            src_ref=mixed_all.at[peer(j)],
            dst_ref=mixed_all.at[peer(j)],
            send_sem=mixed_send.at[j],
            recv_sem=mixed_recv.at[peer(j)],
            device_id=(peer(j), me),
            device_id_type=MESH,
        ).wait_recv()

    each(heads - 1, lambda j: mixed_copy(j).start())

    on = on_ref[0].astype(F32)
    flags = jnp.full((FLAG_ROWS, part.shape[1]), 1.0, F32) * on
    body_rows = pl.ds(0, rows)
    flag_rows = pl.ds(rows, FLAG_ROWS)

    def order(i):
        if isinstance(i, int):
            return i // 2 if i % 2 == 0 else depth - 1 - i // 2
        return jnp.where(i % 2 == 0, i // 2, depth - 1 - i // 2)

    def own_part(rr):
        return part[pl.ds(pl.multiple_of(rr * rows, rows), rows)]

    def core_copy(slot):
        return pltpu.make_async_remote_copy(
            core_out.at[slot], core_in.at[slot], core_out_sem.at[slot], core_in_sem.at[slot],
            device_id=sibling, device_id_type=MESH,
        )

    def x_copy(zz):
        return pltpu.make_async_remote_copy(
            x_out.at[zz], x_in.at[zz], x_out_sem.at[zz], x_in_sem.at[zz],
            device_id=across, device_id_type=MESH,
        )

    def up_copy(zz):
        return pltpu.make_async_remote_copy(
            z_out.at[zz], up_in.at[zz], z_out_sem.at[zz], up_sem.at[zz],
            device_id=above, device_id_type=MESH,
        )

    def down_copy(zz):
        return pltpu.make_async_remote_copy(
            z_out.at[zz], down_in.at[zz], z_out_sem.at[zz], down_sem.at[zz],
            device_id=below, device_id_type=MESH,
        )

    loads[3].wait()
    masked = mixed_all[head] * on.astype(BF16)

    def sum_start(i):
        zz = order(i)
        at = pl.multiple_of(zz * group, group)
        part[pl.ds(at, group)] = dot(cot[:, pl.ds(at, group)], masked, (0, 0))
        for xx in (1 - x, x):
            slot = zz * 2 + xx
            core_out[slot, body_rows] = own_part(rep(zz, xx, 1 - c)).astype(BF16)
            core_out[slot, flag_rows] = flags.astype(BF16)
            core_copy(slot).start()

    def sum_x(i):
        zz = order(i)
        slot = zz * 2 + 1 - x
        core_copy(slot).wait_recv()
        x_out[zz, body_rows] = (
            own_part(rep(zz, 1 - x, c)) + core_in[slot, body_rows].astype(F32)
        ).astype(BF16)
        x_out[zz, flag_rows] = (flags + core_in[slot, flag_rows].astype(F32)).astype(BF16)
        x_copy(zz).start()

    def local_sum(zz):
        slot = zz * 2 + x
        core_copy(slot).wait_recv()
        x_copy(zz).wait_recv()
        main = (
            own_part(rep(zz, x, c))
            + core_in[slot, body_rows].astype(F32)
            + x_in[zz, body_rows].astype(F32)
        )
        flag = (
            flags + core_in[slot, flag_rows].astype(F32) + x_in[zz, flag_rows].astype(F32)
        )
        return main, flag

    def put(dst, zz, main, flag):
        dst[zz, body_rows] = main.astype(BF16)
        dst[zz, flag_rows] = flag.astype(BF16)

    def plus(pair, src, zz):
        return (
            pair[0] + src[zz, body_rows].astype(F32),
            pair[1] + src[zz, flag_rows].astype(F32),
        )

    def sum_z(i):
        zz = jnp.where(z < depth // 2, depth - 1 - order(i), order(i))

        @pl.when(zz > z)
        def _():
            pair = local_sum(zz)

            @pl.when(z == 0)
            def _():
                put(z_out, zz, *pair)

            @pl.when(z > 0)
            def _():
                up_copy(zz).wait_recv()
                put(z_out, zz, *plus(pair, up_in, zz))

            up_copy(zz).start()

        @pl.when(zz < z)
        def _():
            pair = local_sum(zz)

            @pl.when(z == depth - 1)
            def _():
                put(z_out, zz, *pair)

            @pl.when(z < depth - 1)
            def _():
                down_copy(zz).wait_recv()
                put(z_out, zz, *plus(pair, down_in, zz))

            down_copy(zz).start()

    def sum_end():
        main, flag = local_sum(z)
        part[pl.ds(0, rows)] = main
        part[pl.ds(rows, FLAG_ROWS)] = flag

        def add(src, copy):
            copy(z).wait_recv()
            part[pl.ds(0, rows)] += src[z, body_rows].astype(F32)
            part[pl.ds(rows, FLAG_ROWS)] += src[z, flag_rows].astype(F32)

        pl.when(z > 0)(lambda: add(up_in, up_copy))
        pl.when(z < depth - 1)(lambda: add(down_in, down_copy))
        weight_grad_ref[...] = part[pl.ds(0, rows)] / part[pl.ds(rows, 1)]

    def columns(zz):
        return pl.ds(pl.multiple_of(zz * group, group), group)

    def grad_group(d):
        def body(zz, _):
            core_wait(head, zz)
            mixed_grad[...] += dot(cot[:, columns(zz)], w_all[head, columns(zz)], (1, 0))

        around(d, body)

    def layer_copy(zz):
        return pltpu.make_async_copy(
            layer.at[:, columns(zz)], layer_hbm.at[0, :, columns(zz)], layer_sem.at[zz]
        )

    def term(hh, zz):
        return dot(mixed_all[hh], w_all[hh, columns(zz)], (1, 1)).astype(BF16).astype(F32)

    def layer_group(d):
        def body(zz, _):
            each(heads - 1, lambda j: core_wait(peer(j), zz))
            total = term(0, zz)
            if heads <= 4:
                for i in range(1, heads):
                    total = total + term(i, zz)
            else:
                total = lax.fori_loop(1, heads, lambda i, t: t + term(i, zz), total)
            layer[:, columns(zz)] = total.astype(BF16)
            layer_copy(zz).start()

        around(d, body)

    for i in range(depth):
        sum_start(i)
        if i == 0:
            gather_z(1)
        else:
            sum_x(i - 1)
        if i == 2:
            send_x(1)
    gather_x(0)
    sum_x(depth - 1)
    for d in range(2, depth):
        gather_z(d)
        send_x(d)
        gather_x(d - 1)
        sum_z(d - 2)
    mixed_grad[...] = jnp.zeros_like(mixed_grad)
    loads[4].wait()
    gather_x(depth - 1)
    for i in range(depth):
        gather_heads(i)
        if i < 2:
            sum_z(depth - 2 + i)
        grad_group(i)
        if i == 0:
            each(heads - 1, mixed_wait)
        if i > 0:
            layer_group(i - 1)
    value_grad_ref[0] = dot(
        weights_ref[...], mixed_grad[...].astype(BF16), (0, 0)
    ).astype(BF16)
    layer_group(depth - 1)
    sum_end()

    each(depth, lambda i: layer_copy(i).wait())
    each(heads - 1, lambda j: mixed_copy(j).wait_send())

    def drain(zz):
        for xx in (0, 1):
            rr = rep(zz, xx, c)
            each(heads - 1, lambda j: to_peer(j, rr).wait_send())
            each(heads, lambda hh: to_core(hh, rr).wait_send())
            core_copy(zz * 2 + xx).wait_send()
        rr = rep(zz, x, c)
        to_across(rr).wait_send()
        x_copy(zz).wait_send()
        pl.when((zz <= z) & (z < depth - 1))(lambda: to_above(rr).wait_send())
        pl.when((zz >= z) & (z > 0))(lambda: to_below(rr).wait_send())
        pl.when(zz > z)(lambda: up_copy(zz).wait_send())
        pl.when(zz < z)(lambda: down_copy(zz).wait_send())

    each(depth, drain)


def hand_over(pieces, *refs):
    sems = refs[-1]
    copies = []
    for src, dst in zip(refs[:3], refs[3:6]):
        count = pieces if src.shape[-2] * src.shape[-1] > 65536 * pieces else 1
        step = src.shape[-2] // count
        for i in range(count):
            cut = (0,) * (len(src.shape) - 2) + (pl.ds(i * step, step),)
            copies.append(pltpu.make_async_copy(src.at[cut], dst.at[cut], sems.at[len(copies)]))
    for copy in copies:
        copy.start()
    for copy in copies:
        copy.wait()


def local(heads, replicas, queries, keys, values, out_weight, cotangent, on_time):
    _, tokens, features = queries.shape
    value_features = values.shape[2]
    rows = out_weight.shape[0]
    model = cotangent.shape[2]
    depth = replicas // 4
    summed = (rows + FLAG_ROWS, value_features)
    hbm = pl.BlockSpec(memory_space=pltpu.HBM)
    vmem = pl.BlockSpec(memory_space=pltpu.VMEM)
    dma = pltpu.SemaphoreType.DMA
    outputs = pl.pallas_call(
        functools.partial(kernel, heads, replicas),
        out_shape=(
            jax.ShapeDtypeStruct(cotangent.shape, BF16),
            jax.ShapeDtypeStruct(values.shape, BF16),
            jax.ShapeDtypeStruct(out_weight.shape, F32),
        ),
        in_specs=[hbm] * 5 + [pl.BlockSpec(memory_space=pltpu.SMEM)],
        out_specs=(hbm, vmem, vmem),
        scratch_shapes=[
            pltpu.VMEM((tokens, features), BF16),
            pltpu.VMEM((tokens, features), BF16),
            pltpu.VMEM((tokens, value_features), BF16),
            pltpu.VMEM((tokens, model), BF16),
            pltpu.VMEM((tokens, model), BF16),
            pltpu.VMEM((heads, model, value_features), BF16),
            pltpu.VMEM((heads, tokens, value_features), BF16),
            pltpu.VMEM((tokens, value_features), F32),
            pltpu.VMEM((model, value_features), F32),
            pltpu.VMEM((tokens, tokens), BF16),
            pltpu.VMEM((depth * 2,) + summed, BF16),
            pltpu.VMEM((depth * 2,) + summed, BF16),
            pltpu.VMEM((depth,) + summed, BF16),
            pltpu.VMEM((depth,) + summed, BF16),
            pltpu.VMEM((depth,) + summed, BF16),
            pltpu.VMEM((depth,) + summed, BF16),
            pltpu.VMEM((depth,) + summed, BF16),
            dma((5,)),
            dma((depth,)),
            dma((heads, replicas)),
            dma((replicas,)),
            dma((replicas,)),
            dma((replicas,)),
            dma((heads, replicas)),
            dma((heads, replicas)),
            dma((heads,)),
            dma((heads,)),
            dma((depth * 2,)),
            dma((depth * 2,)),
            dma((depth,)),
            dma((depth,)),
            dma((depth,)),
            dma((depth,)),
            dma((depth,)),
        ],
        compiler_params=pltpu.CompilerParams(
            collective_id=0, has_side_effects=True, vmem_limit_bytes=56 * 1024 * 1024
        ),
    )(queries, keys, values, out_weight, cotangent, on_time)
    return pl.pallas_call(
        functools.partial(hand_over, 4),
        out_shape=tuple(jax.ShapeDtypeStruct(o.shape, o.dtype) for o in outputs),
        in_specs=[hbm] * 3,
        out_specs=(hbm,) * 3,
        scratch_shapes=[dma((12,))],
        compiler_params=pltpu.CompilerParams(vmem_limit_bytes=56 * 1024 * 1024),
    )(*outputs)


def solution(mesh):
    return jax.shard_map(
        functools.partial(local, mesh.shape["head"], mesh.shape["replica"]),
        mesh=mesh,
        in_specs=(
            P("replica", None, "head"),
            P("replica", None, "head"),
            P("replica", None, "head"),
            P("replica", "head"),
            P("replica", None, None),
            P("replica"),
        ),
        out_specs=(P("replica", None, None), P("replica", None, "head"), P("replica", "head")),
        check_vma=False,
    )
```

```python
import functools
import math

import jax
import jax.numpy as jnp
from jax import lax
from jax.experimental import pallas as pl
from jax.experimental.pallas import tpu as pltpu
from jax.sharding import PartitionSpec as P

MESH = pl.DeviceIdType.MESH
FLAG_ROWS = 16
F32 = jnp.float32
BF16 = jnp.bfloat16


def dot(a, b, dims):
    return lax.dot_general(a, b, ((dims[:1], dims[1:]), ((), ())), preferred_element_type=F32)


def each(count, body):
    if count <= 4:
        for i in range(count):
            body(i)
    else:
        lax.fori_loop(0, count, lambda i, c: (body(i), c)[1], 0)


def when(cond, body):
    if isinstance(cond, bool):
        if cond:
            body()
    else:
        pl.when(cond)(body)


def kernel(
    heads, replicas,
    q_hbm, k_hbm, v_hbm, w_hbm, cot_hbm, on_ref,
    layer_hbm, value_grad_ref, weight_grad_ref,
    q, k, v, cot, layer, w_all, mixed_all, mixed_grad, part, weights_ref,
    core_out, core_in, x_out, x_in, z_out, up_in, down_in,
    load_sem, layer_sem,
    w_recv, up_send, down_send, x_send, head_send, core_send,
    mixed_send, mixed_recv,
    core_out_sem, core_in_sem, x_out_sem, x_in_sem, z_out_sem, up_sem, down_sem,
):
    depth = replicas // 4
    rows = w_hbm.shape[0]
    group = 4 * rows
    tokens = q.shape[0]
    head = lax.axis_index("head")
    me = lax.axis_index("replica")
    z, x, c = me // 4, (me // 2) % 2, me % 2

    def rep(zz, xx, cc):
        return zz * 4 + xx * 2 + cc

    sibling = (head, rep(z, x, 1 - c))
    across = (head, rep(z, 1 - x, c))
    above = (head, rep(z + 1, x, c))
    below = (head, rep(z - 1, x, c))

    def peer(j):
        return lax.rem(head + 1 + j, heads)

    barrier = pltpu.get_barrier_semaphore()

    def greet(device):
        pl.semaphore_signal(barrier, inc=1, device_id=device, device_id_type=MESH)

    greet(sibling)
    greet(across)
    each(heads - 1, lambda j: greet((peer(j), me)))
    pl.when(z > 0)(lambda: greet(below))
    pl.when(z < depth - 1)(lambda: greet(above))

    loads = [
        pltpu.make_async_copy(src, dst, load_sem.at[i])
        for i, (src, dst) in enumerate(
            ((q_hbm.at[0], q), (k_hbm.at[0], k), (v_hbm.at[0], v), (cot_hbm.at[0], cot),
             (w_hbm, w_all.at[head, pl.ds(pl.multiple_of(me * rows, rows), rows)]))
        )
    ]
    for load in loads:
        load.start()
    pl.semaphore_wait(
        barrier, 1 + heads + jnp.where(z > 0, 1, 0) + jnp.where(z < depth - 1, 1, 0)
    )

    def block(hh, rr):
        return w_all.at[hh, pl.ds(pl.multiple_of(rr * rows, rows), rows)]

    def w_copy(hh, rr, sem, device):
        return pltpu.make_async_remote_copy(
            src_ref=block(hh, rr),
            dst_ref=block(hh, rr),
            send_sem=sem,
            recv_sem=w_recv.at[hh, rr],
            device_id=device,
            device_id_type=MESH,
        )

    def w_wait(hh, rr):
        w_copy(hh, rr, core_send.at[hh, rr], sibling).wait_recv()

    def to_above(hh, rr):
        return w_copy(hh, rr, up_send.at[hh, rr], above)

    def to_below(hh, rr):
        return w_copy(hh, rr, down_send.at[hh, rr], below)

    def to_across(rr):
        return w_copy(head, rr, x_send.at[rr], across)

    def to_peer(j, rr):
        return w_copy(head, rr, head_send.at[j, rr], (peer(j), me))

    def to_core(hh, rr):
        return w_copy(hh, rr, core_send.at[hh, rr], sibling)

    def to_peers(rr):
        each(heads - 1, lambda j: to_peer(j, rr).start())

    def send_up(hh, rr):
        pl.when(z < depth - 1)(lambda: to_above(hh, rr).start())

    def send_down(hh, rr):
        pl.when(z > 0)(lambda: to_below(hh, rr).start())

    loads[4].wait()
    send_up(head, me)
    send_down(head, me)
    to_peers(me)
    to_across(me).start()
    to_core(head, me).start()

    def around(d, body):
        if isinstance(d, int) and d == 0:
            body(z, None)
        else:
            pl.when(z - d >= 0)(lambda: body(z - d, True))
            pl.when(z + d < depth)(lambda: body(z + d, False))

    def gather_y():
        def body(j):
            hh = peer(j)
            w_wait(hh, me)
            send_up(hh, me)
            send_down(hh, me)
            to_core(hh, me).start()

        each(heads - 1, body)

    def gather_z(d):
        def body(zz, went_up):
            rr = rep(zz, x, c)

            def one(j):
                hh = lax.rem(head + j, heads)
                w_wait(hh, rr)
                if went_up:
                    send_up(hh, rr)
                else:
                    send_down(hh, rr)
                to_core(hh, rr).start()

            each(heads, one)

        around(d, body)

    def send_x(d):
        around(d, lambda zz, _: to_across(rep(zz, x, c)).start())

    def gather_x(d):
        def body(zz, _):
            rr = rep(zz, 1 - x, c)
            w_wait(head, rr)
            to_peers(rr)
            to_core(head, rr).start()

        around(d, body)

    def gather_heads(d):
        def body(zz, _):
            rr = rep(zz, 1 - x, c)

            def from_peer(j):
                w_wait(peer(j), rr)
                to_core(peer(j), rr).start()

            each(heads - 1, from_peer)

        around(d, body)

    def core_wait(hh, zz):
        for xx in (0, 1):
            w_wait(hh, rep(zz, xx, 1 - c))

    for load in loads[:3]:
        load.wait()
    row = lax.broadcasted_iota(jnp.int32, (tokens, tokens), 0)
    col = lax.broadcasted_iota(jnp.int32, (tokens, tokens), 1)
    offset = (row - col).astype(F32)
    log_gamma = jnp.float32(math.log(1.0 - 2.0 ** -5.0))
    for i in range(1, heads):
        log_gamma = jnp.where(head == i, jnp.float32(math.log(1.0 - 2.0 ** (-5.0 - i))), log_gamma)
    decay = jnp.where(offset >= 0.0, jnp.exp(jnp.maximum(offset, 0.0) * log_gamma), 0.0)
    scores = dot(q[...], k[...], (1, 1)) * decay
    denom = jnp.maximum(jnp.sum(jnp.abs(scores), axis=-1, keepdims=True), 1.0)
    weights_ref[...] = (scores / denom).astype(BF16)
    mixed_all[head] = dot(weights_ref[...], v[...], (1, 0)).astype(BF16)

    def mixed_copy(j):
        return pltpu.make_async_remote_copy(
            src_ref=mixed_all.at[head],
            dst_ref=mixed_all.at[head],
            send_sem=mixed_send.at[j],
            recv_sem=mixed_recv.at[head],
            device_id=(peer(j), me),
            device_id_type=MESH,
        )

    def mixed_wait(j):
        pltpu.make_async_remote_copy(
            src_ref=mixed_all.at[peer(j)],
            dst_ref=mixed_all.at[peer(j)],
            send_sem=mixed_send.at[j],
            recv_sem=mixed_recv.at[peer(j)],
            device_id=(peer(j), me),
            device_id_type=MESH,
        ).wait_recv()

    each(heads - 1, lambda j: mixed_copy(j).start())

    on = on_ref[0].astype(F32)
    flags = jnp.full((FLAG_ROWS, part.shape[1]), 1.0, F32) * on
    body_rows = pl.ds(0, rows)
    flag_rows = pl.ds(rows, FLAG_ROWS)

    def order(i):
        if isinstance(i, int):
            return i // 2 if i % 2 == 0 else depth - 1 - i // 2
        return jnp.where(i % 2 == 0, i // 2, depth - 1 - i // 2)

    def own_part(rr):
        return part[pl.ds(pl.multiple_of(rr * rows, rows), rows)]

    def core_copy(slot):
        return pltpu.make_async_remote_copy(
            core_out.at[slot], core_in.at[slot], core_out_sem.at[slot], core_in_sem.at[slot],
            device_id=sibling, device_id_type=MESH,
        )

    def x_copy(zz):
        return pltpu.make_async_remote_copy(
            x_out.at[zz], x_in.at[zz], x_out_sem.at[zz], x_in_sem.at[zz],
            device_id=across, device_id_type=MESH,
        )

    def up_copy(zz):
        return pltpu.make_async_remote_copy(
            z_out.at[zz], up_in.at[zz], z_out_sem.at[zz], up_sem.at[zz],
            device_id=above, device_id_type=MESH,
        )

    def down_copy(zz):
        return pltpu.make_async_remote_copy(
            z_out.at[zz], down_in.at[zz], z_out_sem.at[zz], down_sem.at[zz],
            device_id=below, device_id_type=MESH,
        )

    loads[3].wait()
    masked = mixed_all[head] * on.astype(BF16)

    def sum_start(i):
        zz = order(i)
        at = pl.multiple_of(zz * group, group)
        part[pl.ds(at, group)] = dot(cot[:, pl.ds(at, group)], masked, (0, 0))
        for xx in (1 - x, x):
            slot = zz * 2 + xx
            core_out[slot, body_rows] = own_part(rep(zz, xx, 1 - c)).astype(BF16)
            core_out[slot, flag_rows] = flags.astype(BF16)
            core_copy(slot).start()

    def sum_x(i):
        zz = order(i)
        slot = zz * 2 + 1 - x
        core_copy(slot).wait_recv()
        x_out[zz, body_rows] = (
            own_part(rep(zz, 1 - x, c)) + core_in[slot, body_rows].astype(F32)
        ).astype(BF16)
        x_out[zz, flag_rows] = (flags + core_in[slot, flag_rows].astype(F32)).astype(BF16)
        x_copy(zz).start()

    def local_sum(zz):
        slot = zz * 2 + x
        core_copy(slot).wait_recv()
        x_copy(zz).wait_recv()
        main = (
            own_part(rep(zz, x, c))
            + core_in[slot, body_rows].astype(F32)
            + x_in[zz, body_rows].astype(F32)
        )
        flag = (
            flags + core_in[slot, flag_rows].astype(F32) + x_in[zz, flag_rows].astype(F32)
        )
        return main, flag

    def put(dst, zz, main, flag):
        dst[zz, body_rows] = main.astype(BF16)
        dst[zz, flag_rows] = flag.astype(BF16)

    def plus(pair, src, zz):
        return (
            pair[0] + src[zz, body_rows].astype(F32),
            pair[1] + src[zz, flag_rows].astype(F32),
        )

    def sum_z(i):
        zz = jnp.where(z < depth // 2, depth - 1 - order(i), order(i))

        @pl.when(zz > z)
        def _():
            pair = local_sum(zz)

            @pl.when(z == 0)
            def _():
                put(z_out, zz, *pair)

            @pl.when(z > 0)
            def _():
                up_copy(zz).wait_recv()
                put(z_out, zz, *plus(pair, up_in, zz))

            up_copy(zz).start()

        @pl.when(zz < z)
        def _():
            pair = local_sum(zz)

            @pl.when(z == depth - 1)
            def _():
                put(z_out, zz, *pair)

            @pl.when(z < depth - 1)
            def _():
                down_copy(zz).wait_recv()
                put(z_out, zz, *plus(pair, down_in, zz))

            down_copy(zz).start()

    def sum_end():
        main, flag = local_sum(z)
        part[pl.ds(0, rows)] = main
        part[pl.ds(rows, FLAG_ROWS)] = flag

        def add(src, copy):
            copy(z).wait_recv()
            part[pl.ds(0, rows)] += src[z, body_rows].astype(F32)
            part[pl.ds(rows, FLAG_ROWS)] += src[z, flag_rows].astype(F32)

        pl.when(z > 0)(lambda: add(up_in, up_copy))
        pl.when(z < depth - 1)(lambda: add(down_in, down_copy))
        weight_grad_ref[...] = part[pl.ds(0, rows)] / part[pl.ds(rows, 1)]

    def columns(zz):
        return pl.ds(pl.multiple_of(zz * group, group), group)

    def grad_group(d):
        def body(zz, _):
            core_wait(head, zz)
            mixed_grad[...] += dot(cot[:, columns(zz)], w_all[head, columns(zz)], (1, 0))

        around(d, body)

    def layer_copy(zz):
        return pltpu.make_async_copy(
            layer.at[:, columns(zz)], layer_hbm.at[0, :, columns(zz)], layer_sem.at[zz]
        )

    def term(hh, zz):
        return dot(mixed_all[hh], w_all[hh, columns(zz)], (1, 1)).astype(BF16).astype(F32)

    def layer_group(d):
        def body(zz, _):
            each(heads - 1, lambda j: core_wait(peer(j), zz))
            total = term(0, zz)
            if heads <= 4:
                for i in range(1, heads):
                    total = total + term(i, zz)
            else:
                total = lax.fori_loop(1, heads, lambda i, t: t + term(i, zz), total)
            layer[:, columns(zz)] = total.astype(BF16)
            layer_copy(zz).start()

        around(d, body)

    gather_y()
    gather_z(1)
    for i in range(depth):
        sum_start(i)
        if i == 1:
            gather_x(0)
        if i > 0:
            sum_x(i - 1)
        if i == 2:
            send_x(1)
    sum_x(depth - 1)
    mixed_grad[...] = jnp.zeros_like(mixed_grad)
    for d in range(2, depth):
        gather_z(d)
        sum_z(d - 2)
        gather_x(d - 1)
        send_x(d)
    for i in range(depth):
        gather_heads(i)
        grad_group(i)
        if i < 2:
            sum_z(depth - 2 + i)
        if i == 0:
            gather_x(depth - 1)
            each(heads - 1, mixed_wait)
        if i > 0:
            layer_group(i - 1)
    value_grad_ref[0] = dot(
        weights_ref[...], mixed_grad[...].astype(BF16), (0, 0)
    ).astype(BF16)
    layer_group(depth - 1)
    sum_end()

    each(depth, lambda i: layer_copy(i).wait())
    each(heads - 1, lambda j: mixed_copy(j).wait_send())

    def drain(zz):
        rr = rep(zz, x, c)
        far = rep(zz, 1 - x, c)

        def one(hh):
            to_core(hh, rr).wait_send()
            to_core(hh, far).wait_send()
            pl.when((zz <= z) & (z < depth - 1))(lambda: to_above(hh, rr).wait_send())
            pl.when((zz >= z) & (z > 0))(lambda: to_below(hh, rr).wait_send())

        each(heads, one)
        each(heads - 1, lambda j: to_peer(j, far).wait_send())
        to_across(rr).wait_send()
        core_copy(zz * 2).wait_send()
        core_copy(zz * 2 + 1).wait_send()
        x_copy(zz).wait_send()
        pl.when(zz > z)(lambda: up_copy(zz).wait_send())
        pl.when(zz < z)(lambda: down_copy(zz).wait_send())

    each(heads - 1, lambda j: to_peer(j, me).wait_send())
    each(depth, drain)


def hand_over(pieces, *refs):
    load_sem, store_sem = refs[-2:]
    moves = []
    for src, dst, held in zip(refs[:3], refs[3:6], refs[6:9]):
        count = pieces if src.shape[-2] * src.shape[-1] > 65536 * pieces else 1
        step = src.shape[-2] // count
        for i in range(count):
            cut = (0,) * (len(src.shape) - 2) + (pl.ds(i * step, step),)
            n = len(moves)
            moves.append((
                pltpu.make_async_copy(src.at[cut], held.at[cut], load_sem.at[n]),
                pltpu.make_async_copy(held.at[cut], dst.at[cut], store_sem.at[n]),
            ))
    for load, _ in moves:
        load.start()
    for load, store in moves:
        load.wait()
        store.start()
    for _, store in moves:
        store.wait()


def local(heads, replicas, queries, keys, values, out_weight, cotangent, on_time):
    _, tokens, features = queries.shape
    value_features = values.shape[2]
    rows = out_weight.shape[0]
    model = cotangent.shape[2]
    depth = replicas // 4
    summed = (rows + FLAG_ROWS, value_features)
    hbm = pl.BlockSpec(memory_space=pltpu.HBM)
    vmem = pl.BlockSpec(memory_space=pltpu.VMEM)
    dma = pltpu.SemaphoreType.DMA
    outputs = pl.pallas_call(
        functools.partial(kernel, heads, replicas),
        out_shape=(
            jax.ShapeDtypeStruct(cotangent.shape, BF16),
            jax.ShapeDtypeStruct(values.shape, BF16),
            jax.ShapeDtypeStruct(out_weight.shape, F32),
        ),
        in_specs=[hbm] * 5 + [pl.BlockSpec(memory_space=pltpu.SMEM)],
        out_specs=(hbm, vmem, vmem),
        scratch_shapes=[
            pltpu.VMEM((tokens, features), BF16),
            pltpu.VMEM((tokens, features), BF16),
            pltpu.VMEM((tokens, value_features), BF16),
            pltpu.VMEM((tokens, model), BF16),
            pltpu.VMEM((tokens, model), BF16),
            pltpu.VMEM((heads, model, value_features), BF16),
            pltpu.VMEM((heads, tokens, value_features), BF16),
            pltpu.VMEM((tokens, value_features), F32),
            pltpu.VMEM((model, value_features), F32),
            pltpu.VMEM((tokens, tokens), BF16),
            pltpu.VMEM((depth * 2,) + summed, BF16),
            pltpu.VMEM((depth * 2,) + summed, BF16),
            pltpu.VMEM((depth,) + summed, BF16),
            pltpu.VMEM((depth,) + summed, BF16),
            pltpu.VMEM((depth,) + summed, BF16),
            pltpu.VMEM((depth,) + summed, BF16),
            pltpu.VMEM((depth,) + summed, BF16),
            dma((5,)),
            dma((depth,)),
            dma((heads, replicas)),
            dma((heads, replicas)),
            dma((heads, replicas)),
            dma((replicas,)),
            dma((heads, replicas)),
            dma((heads, replicas)),
            dma((heads,)),
            dma((heads,)),
            dma((depth * 2,)),
            dma((depth * 2,)),
            dma((depth,)),
            dma((depth,)),
            dma((depth,)),
            dma((depth,)),
            dma((depth,)),
        ],
        compiler_params=pltpu.CompilerParams(
            collective_id=0, has_side_effects=True, vmem_limit_bytes=56 * 1024 * 1024
        ),
    )(queries, keys, values, out_weight, cotangent, on_time)
    return pl.pallas_call(
        functools.partial(hand_over, 8),
        out_shape=tuple(jax.ShapeDtypeStruct(o.shape, o.dtype) for o in outputs),
        in_specs=[hbm] * 3,
        out_specs=(hbm,) * 3,
        scratch_shapes=[pltpu.VMEM(o.shape, o.dtype) for o in outputs] + [dma((10,)), dma((10,))],
        compiler_params=pltpu.CompilerParams(vmem_limit_bytes=56 * 1024 * 1024),
    )(*outputs)


def solution(mesh):
    return jax.shard_map(
        functools.partial(local, mesh.shape["head"], mesh.shape["replica"]),
        mesh=mesh,
        in_specs=(
            P("replica", None, "head"),
            P("replica", None, "head"),
            P("replica", None, "head"),
            P("replica", "head"),
            P("replica", None, None),
            P("replica"),
        ),
        out_specs=(P("replica", None, None), P("replica", None, "head"), P("replica", "head")),
        check_vma=False,
    )
```

```python
import functools
import math

import jax
import jax.numpy as jnp
from jax import lax
from jax.experimental import pallas as pl
from jax.experimental.pallas import tpu as pltpu
from jax.sharding import PartitionSpec as P

MESH = pl.DeviceIdType.MESH
FLAG_ROWS = 16
F32 = jnp.float32
BF16 = jnp.bfloat16


def dot(a, b, dims):
    return lax.dot_general(a, b, ((dims[:1], dims[1:]), ((), ())), preferred_element_type=F32)


def each(count, body):
    if count <= 4:
        for i in range(count):
            body(i)
    else:
        lax.fori_loop(0, count, lambda i, c: (body(i), c)[1], 0)


def when(cond, body):
    if isinstance(cond, bool):
        if cond:
            body()
    else:
        pl.when(cond)(body)


def kernel(
    heads, replicas,
    q_hbm, k_hbm, v_hbm, w_hbm, cot_hbm, on_ref,
    layer_hbm, value_grad_ref, weight_grad_ref,
    q, k, v, cot, layer, w_all, mixed_all, mixed_grad, part, weights_ref,
    core_out, core_in, x_out, x_in, z_out, z_in,
    load_sem, layer_sem,
    w_recv, line_send, x_send, head_send, core_send,
    mixed_send, mixed_recv,
    core_out_sem, core_in_sem, x_out_sem, x_in_sem, z_out_sem, z_in_sem,
):
    depth = replicas // 4
    rows = w_hbm.shape[0]
    group = 4 * rows
    tokens = q.shape[0]
    head = lax.axis_index("head")
    me = lax.axis_index("replica")
    z, x, c = me // 4, (me // 2) % 2, me % 2

    def rep(zz, xx, cc):
        return zz * 4 + xx * 2 + cc

    sibling = (head, rep(z, x, 1 - c))
    across = (head, rep(z, 1 - x, c))

    def line(zz):
        return (head, rep(zz, x, c))

    def peer(j):
        return lax.rem(head + 1 + j, heads)

    barrier = pltpu.get_barrier_semaphore()

    def greet(device):
        pl.semaphore_signal(barrier, inc=1, device_id=device, device_id_type=MESH)

    greet(sibling)
    greet(across)
    each(heads - 1, lambda j: greet((peer(j), me)))
    each(depth, lambda zz: pl.when(zz != z)(lambda: greet(line(zz))))

    loads = [
        pltpu.make_async_copy(src, dst, load_sem.at[i])
        for i, (src, dst) in enumerate(
            ((q_hbm.at[0], q), (k_hbm.at[0], k), (v_hbm.at[0], v), (cot_hbm.at[0], cot),
             (w_hbm, w_all.at[head, pl.ds(pl.multiple_of(me * rows, rows), rows)]))
        )
    ]
    for load in loads:
        load.start()
    pl.semaphore_wait(barrier, heads + depth)

    def block(hh, rr):
        return w_all.at[hh, pl.ds(pl.multiple_of(rr * rows, rows), rows)]

    def w_copy(hh, rr, sem, device):
        return pltpu.make_async_remote_copy(
            src_ref=block(hh, rr),
            dst_ref=block(hh, rr),
            send_sem=sem,
            recv_sem=w_recv.at[hh, rr],
            device_id=device,
            device_id_type=MESH,
        )

    def w_wait(hh, rr):
        w_copy(hh, rr, core_send.at[hh, rr], sibling).wait_recv()

    def to_line(zz):
        return w_copy(head, me, line_send.at[zz], line(zz))

    def to_across(rr):
        return w_copy(head, rr, x_send.at[rr], across)

    def to_peer(j, rr):
        return w_copy(head, rr, head_send.at[j, rr], (peer(j), me))

    def to_core(hh, rr):
        return w_copy(hh, rr, core_send.at[hh, rr], sibling)

    def to_peers(rr):
        each(heads - 1, lambda j: to_peer(j, rr).start())

    def around(d, body):
        if isinstance(d, int) and d == 0:
            body(z)
        else:
            pl.when(z - d >= 0)(lambda: body(z - d))
            pl.when(z + d < depth)(lambda: body(z + d))

    def send_line(d):
        around(d, lambda zz: to_line(zz).start())

    loads[4].wait()
    send_line(1)
    to_peers(me)
    to_across(me).start()
    to_core(head, me).start()

    def gather_z(d):
        def body(zz):
            rr = rep(zz, x, c)
            w_wait(head, rr)
            to_peers(rr)
            to_across(rr).start()
            to_core(head, rr).start()

        around(d, body)

    def gather_x(d):
        def body(zz):
            rr = rep(zz, 1 - x, c)
            w_wait(head, rr)
            to_peers(rr)
            to_core(head, rr).start()

        around(d, body)

    def gather_heads(d):
        def body(zz):
            def from_peer(j):
                for xx in (x, 1 - x):
                    w_wait(peer(j), rep(zz, xx, c))
                    to_core(peer(j), rep(zz, xx, c)).start()

            each(heads - 1, from_peer)

        around(d, body)

    def core_wait(hh, zz):
        for xx in (0, 1):
            w_wait(hh, rep(zz, xx, 1 - c))

    for load in loads[:3]:
        load.wait()
    row = lax.broadcasted_iota(jnp.int32, (tokens, tokens), 0)
    col = lax.broadcasted_iota(jnp.int32, (tokens, tokens), 1)
    offset = (row - col).astype(F32)
    log_gamma = jnp.float32(math.log(1.0 - 2.0 ** -5.0))
    for i in range(1, heads):
        log_gamma = jnp.where(head == i, jnp.float32(math.log(1.0 - 2.0 ** (-5.0 - i))), log_gamma)
    decay = jnp.where(offset >= 0.0, jnp.exp(jnp.maximum(offset, 0.0) * log_gamma), 0.0)
    scores = dot(q[...], k[...], (1, 1)) * decay
    denom = jnp.maximum(jnp.sum(jnp.abs(scores), axis=-1, keepdims=True), 1.0)
    weights_ref[...] = (scores / denom).astype(BF16)
    mixed_all[head] = dot(weights_ref[...], v[...], (1, 0)).astype(BF16)

    def mixed_copy(j):
        return pltpu.make_async_remote_copy(
            src_ref=mixed_all.at[head],
            dst_ref=mixed_all.at[head],
            send_sem=mixed_send.at[j],
            recv_sem=mixed_recv.at[head],
            device_id=(peer(j), me),
            device_id_type=MESH,
        )

    def mixed_wait(j):
        pltpu.make_async_remote_copy(
            src_ref=mixed_all.at[peer(j)],
            dst_ref=mixed_all.at[peer(j)],
            send_sem=mixed_send.at[j],
            recv_sem=mixed_recv.at[peer(j)],
            device_id=(peer(j), me),
            device_id_type=MESH,
        ).wait_recv()

    each(heads - 1, lambda j: mixed_copy(j).start())

    on = on_ref[0].astype(F32)
    flags = jnp.full((FLAG_ROWS, part.shape[1]), 1.0, F32) * on
    body_rows = pl.ds(0, rows)
    flag_rows = pl.ds(rows, FLAG_ROWS)

    def order(i):
        if isinstance(i, int):
            return i // 2 if i % 2 == 0 else depth - 1 - i // 2
        return jnp.where(i % 2 == 0, i // 2, depth - 1 - i // 2)

    def own_part(rr):
        return part[pl.ds(pl.multiple_of(rr * rows, rows), rows)]

    def core_copy(slot):
        return pltpu.make_async_remote_copy(
            core_out.at[slot], core_in.at[slot], core_out_sem.at[slot], core_in_sem.at[slot],
            device_id=sibling, device_id_type=MESH,
        )

    def x_copy(zz):
        return pltpu.make_async_remote_copy(
            x_out.at[zz], x_in.at[zz], x_out_sem.at[zz], x_in_sem.at[zz],
            device_id=across, device_id_type=MESH,
        )

    def z_copy(zz, source, other):
        return pltpu.make_async_remote_copy(
            z_out.at[zz], z_in.at[source], z_out_sem.at[zz], z_in_sem.at[source],
            device_id=line(other), device_id_type=MESH,
        )

    loads[3].wait()
    masked = mixed_all[head] * on.astype(BF16)

    def sum_start(i):
        zz = order(i)
        at = pl.multiple_of(zz * group, group)
        part[pl.ds(at, group)] = dot(cot[:, pl.ds(at, group)], masked, (0, 0))
        for xx in (1 - x, x):
            slot = zz * 2 + xx
            core_out[slot, body_rows] = own_part(rep(zz, xx, 1 - c)).astype(BF16)
            core_out[slot, flag_rows] = flags.astype(BF16)
            core_copy(slot).start()

    def sum_x(i):
        zz = order(i)
        slot = zz * 2 + 1 - x
        core_copy(slot).wait_recv()
        x_out[zz, body_rows] = (
            own_part(rep(zz, 1 - x, c)) + core_in[slot, body_rows].astype(F32)
        ).astype(BF16)
        x_out[zz, flag_rows] = (flags + core_in[slot, flag_rows].astype(F32)).astype(BF16)
        x_copy(zz).start()

    def local_sum(zz):
        slot = zz * 2 + x
        core_copy(slot).wait_recv()
        x_copy(zz).wait_recv()
        main = (
            own_part(rep(zz, x, c))
            + core_in[slot, body_rows].astype(F32)
            + x_in[zz, body_rows].astype(F32)
        )
        flag = (
            flags + core_in[slot, flag_rows].astype(F32) + x_in[zz, flag_rows].astype(F32)
        )
        return main, flag

    def sum_z(i):
        zz = order(i)

        @pl.when(zz != z)
        def _():
            main, flag = local_sum(zz)
            z_out[zz, body_rows] = main.astype(BF16)
            z_out[zz, flag_rows] = flag.astype(BF16)
            z_copy(zz, z, zz).start()

    def sum_end():
        main, flag = local_sum(z)
        part[pl.ds(0, rows)] = main
        part[pl.ds(rows, FLAG_ROWS)] = flag

        def add(source):
            @pl.when(source != z)
            def _():
                z_copy(z, source, source).wait_recv()
                part[pl.ds(0, rows)] += z_in[source, body_rows].astype(F32)
                part[pl.ds(rows, FLAG_ROWS)] += z_in[source, flag_rows].astype(F32)

        each(depth, add)
        weight_grad_ref[...] = part[pl.ds(0, rows)] / part[pl.ds(rows, 1)]

    def columns(zz):
        return pl.ds(pl.multiple_of(zz * group, group), group)

    def grad_group(d):
        def body(zz):
            core_wait(head, zz)
            mixed_grad[...] += dot(cot[:, columns(zz)], w_all[head, columns(zz)], (1, 0))

        around(d, body)

    def layer_copy(zz):
        return pltpu.make_async_copy(
            layer.at[:, columns(zz)], layer_hbm.at[0, :, columns(zz)], layer_sem.at[zz]
        )

    def term(hh, zz):
        return dot(mixed_all[hh], w_all[hh, columns(zz)], (1, 1)).astype(BF16).astype(F32)

    def layer_group(d):
        def body(zz):
            each(heads - 1, lambda j: core_wait(peer(j), zz))
            total = term(0, zz)
            if heads <= 4:
                for i in range(1, heads):
                    total = total + term(i, zz)
            else:
                total = lax.fori_loop(1, heads, lambda i, t: t + term(i, zz), total)
            layer[:, columns(zz)] = total.astype(BF16)
            layer_copy(zz).start()

        around(d, body)

    for d in range(2, depth):
        send_line(d)
    gather_z(1)
    for i in range(depth):
        sum_start(i)
        if i == 1:
            gather_x(0)
        if i > 0:
            sum_x(i - 1)
    sum_x(depth - 1)
    mixed_grad[...] = jnp.zeros_like(mixed_grad)
    for d in range(2, depth):
        gather_z(d)
        sum_z(d - 2)
        gather_x(d - 1)
    sum_z(depth - 2)
    sum_z(depth - 1)
    each(heads - 1, mixed_wait)
    for i in range(depth):
        gather_heads(i)
        grad_group(i)
        if i == 0:
            gather_x(depth - 1)
        if i < depth - 1:
            layer_group(i)
    value_grad_ref[0] = dot(
        weights_ref[...], mixed_grad[...].astype(BF16), (0, 0)
    ).astype(BF16)
    sum_end()
    layer_group(depth - 1)

    each(depth, lambda i: layer_copy(i).wait())
    each(heads - 1, lambda j: mixed_copy(j).wait_send())

    def drain(zz):
        rr = rep(zz, x, c)
        far = rep(zz, 1 - x, c)

        def one(hh):
            to_core(hh, rr).wait_send()
            to_core(hh, far).wait_send()

        each(heads, one)
        each(heads - 1, lambda j: to_peer(j, rr).wait_send())
        each(heads - 1, lambda j: to_peer(j, far).wait_send())
        to_across(rr).wait_send()
        core_copy(zz * 2).wait_send()
        core_copy(zz * 2 + 1).wait_send()
        x_copy(zz).wait_send()

        @pl.when(zz != z)
        def _():
            to_line(zz).wait_send()
            z_copy(zz, z, zz).wait_send()

    each(depth, drain)


def hand_over(pieces, *refs):
    load_sem, store_sem = refs[-2:]
    moves = []
    for src, dst, held in zip(refs[:3], refs[3:6], refs[6:9]):
        count = pieces if src.shape[-2] * src.shape[-1] > 65536 * pieces else 1
        step = src.shape[-2] // count
        for i in range(count):
            cut = (0,) * (len(src.shape) - 2) + (pl.ds(i * step, step),)
            n = len(moves)
            moves.append((
                pltpu.make_async_copy(src.at[cut], held.at[cut], load_sem.at[n]),
                pltpu.make_async_copy(held.at[cut], dst.at[cut], store_sem.at[n]),
            ))
    for load, _ in moves:
        load.start()
    for load, store in moves:
        load.wait()
        store.start()
    for _, store in moves:
        store.wait()


def local(heads, replicas, queries, keys, values, out_weight, cotangent, on_time):
    _, tokens, features = queries.shape
    value_features = values.shape[2]
    rows = out_weight.shape[0]
    model = cotangent.shape[2]
    depth = replicas // 4
    summed = (rows + FLAG_ROWS, value_features)
    hbm = pl.BlockSpec(memory_space=pltpu.HBM)
    vmem = pl.BlockSpec(memory_space=pltpu.VMEM)
    dma = pltpu.SemaphoreType.DMA
    outputs = pl.pallas_call(
        functools.partial(kernel, heads, replicas),
        out_shape=(
            jax.ShapeDtypeStruct(cotangent.shape, BF16),
            jax.ShapeDtypeStruct(values.shape, BF16),
            jax.ShapeDtypeStruct(out_weight.shape, F32),
        ),
        in_specs=[hbm] * 5 + [pl.BlockSpec(memory_space=pltpu.SMEM)],
        out_specs=(hbm, vmem, vmem),
        scratch_shapes=[
            pltpu.VMEM((tokens, features), BF16),
            pltpu.VMEM((tokens, features), BF16),
            pltpu.VMEM((tokens, value_features), BF16),
            pltpu.VMEM((tokens, model), BF16),
            pltpu.VMEM((tokens, model), BF16),
            pltpu.VMEM((heads, model, value_features), BF16),
            pltpu.VMEM((heads, tokens, value_features), BF16),
            pltpu.VMEM((tokens, value_features), F32),
            pltpu.VMEM((model, value_features), F32),
            pltpu.VMEM((tokens, tokens), BF16),
            pltpu.VMEM((depth * 2,) + summed, BF16),
            pltpu.VMEM((depth * 2,) + summed, BF16),
            pltpu.VMEM((depth,) + summed, BF16),
            pltpu.VMEM((depth,) + summed, BF16),
            pltpu.VMEM((depth,) + summed, BF16),
            pltpu.VMEM((depth,) + summed, BF16),
            dma((5,)),
            dma((depth,)),
            dma((heads, replicas)),
            dma((depth,)),
            dma((replicas,)),
            dma((heads, replicas)),
            dma((heads, replicas)),
            dma((heads,)),
            dma((heads,)),
            dma((depth * 2,)),
            dma((depth * 2,)),
            dma((depth,)),
            dma((depth,)),
            dma((depth,)),
            dma((depth,)),
        ],
        compiler_params=pltpu.CompilerParams(
            collective_id=0, has_side_effects=True, vmem_limit_bytes=56 * 1024 * 1024
        ),
    )(queries, keys, values, out_weight, cotangent, on_time)
    return pl.pallas_call(
        functools.partial(hand_over, 8),
        out_shape=tuple(jax.ShapeDtypeStruct(o.shape, o.dtype) for o in outputs),
        in_specs=[hbm] * 3,
        out_specs=(hbm,) * 3,
        scratch_shapes=[pltpu.VMEM(o.shape, o.dtype) for o in outputs] + [dma((10,)), dma((10,))],
        compiler_params=pltpu.CompilerParams(vmem_limit_bytes=56 * 1024 * 1024),
    )(*outputs)


def solution(mesh):
    return jax.shard_map(
        functools.partial(local, mesh.shape["head"], mesh.shape["replica"]),
        mesh=mesh,
        in_specs=(
            P("replica", None, "head"),
            P("replica", None, "head"),
            P("replica", None, "head"),
            P("replica", "head"),
            P("replica", None, None),
            P("replica"),
        ),
        out_specs=(P("replica", None, None), P("replica", None, "head"), P("replica", "head")),
        check_vma=False,
    )
```

```python
import functools
import math

import jax
import jax.numpy as jnp
from jax import lax
from jax.experimental import pallas as pl
from jax.experimental.pallas import tpu as pltpu
from jax.sharding import PartitionSpec as P

MESH = pl.DeviceIdType.MESH
FLAG_ROWS = 16
F32 = jnp.float32
BF16 = jnp.bfloat16


def dot(a, b, dims):
    return lax.dot_general(a, b, ((dims[:1], dims[1:]), ((), ())), preferred_element_type=F32)


def each(count, body):
    if count <= 4:
        for i in range(count):
            body(i)
    else:
        lax.fori_loop(0, count, lambda i, c: (body(i), c)[1], 0)


def when(cond, body):
    if isinstance(cond, bool):
        if cond:
            body()
    else:
        pl.when(cond)(body)


def kernel(
    heads, replicas,
    q_hbm, k_hbm, v_hbm, w_hbm, cot_hbm, on_ref,
    layer_hbm, value_grad_ref, weight_grad_ref,
    q, k, v, cot, layer, w_all, mixed_all, mixed_grad, part, total, weights_ref,
    core_out, core_in, x_out, x_in, z_out, z_in,
    load_sem, layer_sem,
    w_recv, line_send, x_send, head_send, core_send,
    mixed_send, mixed_recv,
    core_out_sem, core_in_sem, x_out_sem, x_in_sem, z_out_sem, z_in_sem,
):
    depth = replicas // 4
    rows = w_hbm.shape[0]
    group = 4 * rows
    tokens = q.shape[0]
    head = lax.axis_index("head")
    me = lax.axis_index("replica")
    z, x, c = me // 4, (me // 2) % 2, me % 2

    def rep(zz, xx, cc):
        return zz * 4 + xx * 2 + cc

    sibling = (head, rep(z, x, 1 - c))
    across = (head, rep(z, 1 - x, c))

    def line(zz):
        return (head, rep(zz, x, c))

    def peer(j):
        return lax.rem(head + 1 + j, heads)

    barrier = pltpu.get_barrier_semaphore()

    def greet(device):
        pl.semaphore_signal(barrier, inc=1, device_id=device, device_id_type=MESH)

    greet(sibling)
    greet(across)
    each(heads - 1, lambda j: greet((peer(j), me)))
    each(depth, lambda zz: pl.when(zz != z)(lambda: greet(line(zz))))

    loads = [
        pltpu.make_async_copy(src, dst, load_sem.at[i])
        for i, (src, dst) in enumerate(
            ((q_hbm.at[0], q), (k_hbm.at[0], k), (v_hbm.at[0], v), (cot_hbm.at[0], cot),
             (w_hbm, w_all.at[head, pl.ds(pl.multiple_of(me * rows, rows), rows)]))
        )
    ]
    for load in loads:
        load.start()
    pl.semaphore_wait(barrier, heads + depth)

    def block(hh, rr):
        return w_all.at[hh, pl.ds(pl.multiple_of(rr * rows, rows), rows)]

    def w_copy(hh, rr, sem, device):
        return pltpu.make_async_remote_copy(
            src_ref=block(hh, rr),
            dst_ref=block(hh, rr),
            send_sem=sem,
            recv_sem=w_recv.at[hh, rr],
            device_id=device,
            device_id_type=MESH,
        )

    def w_wait(hh, rr):
        w_copy(hh, rr, core_send.at[hh, rr], sibling).wait_recv()

    def to_line(zz):
        return w_copy(head, me, line_send.at[zz], line(zz))

    def to_across(rr):
        return w_copy(head, rr, x_send.at[rr], across)

    def to_peer(j, rr):
        return w_copy(head, rr, head_send.at[j, rr], (peer(j), me))

    def to_core(hh, rr):
        return w_copy(hh, rr, core_send.at[hh, rr], sibling)

    def to_peers(rr):
        each(heads - 1, lambda j: to_peer(j, rr).start())

    def around(d, body):
        if isinstance(d, int) and d == 0:
            body(z)
        else:
            pl.when(z - d >= 0)(lambda: body(z - d))
            pl.when(z + d < depth)(lambda: body(z + d))

    def send_line(d):
        around(d, lambda zz: to_line(zz).start())

    loads[4].wait()
    send_line(1)
    to_peers(me)
    to_across(me).start()
    to_core(head, me).start()

    def gather_z(d):
        def body(zz):
            rr = rep(zz, x, c)
            w_wait(head, rr)
            to_peers(rr)
            to_across(rr).start()
            to_core(head, rr).start()

        around(d, body)

    def gather_x(d):
        def body(zz):
            rr = rep(zz, 1 - x, c)
            w_wait(head, rr)
            to_peers(rr)
            to_core(head, rr).start()

        around(d, body)

    def gather_heads(d):
        def body(zz):
            def from_peer(j):
                for xx in (x, 1 - x):
                    w_wait(peer(j), rep(zz, xx, c))
                    to_core(peer(j), rep(zz, xx, c)).start()

            each(heads - 1, from_peer)

        around(d, body)

    def core_wait(hh, zz):
        for xx in (0, 1):
            w_wait(hh, rep(zz, xx, 1 - c))

    for load in loads[:3]:
        load.wait()
    row = lax.broadcasted_iota(jnp.int32, (tokens, tokens), 0)
    col = lax.broadcasted_iota(jnp.int32, (tokens, tokens), 1)
    offset = (row - col).astype(F32)
    log_gamma = jnp.float32(math.log(1.0 - 2.0 ** -5.0))
    for i in range(1, heads):
        log_gamma = jnp.where(head == i, jnp.float32(math.log(1.0 - 2.0 ** (-5.0 - i))), log_gamma)
    decay = jnp.where(offset >= 0.0, jnp.exp(jnp.maximum(offset, 0.0) * log_gamma), 0.0)
    scores = dot(q[...], k[...], (1, 1)) * decay
    denom = jnp.maximum(jnp.sum(jnp.abs(scores), axis=-1, keepdims=True), 1.0)
    weights_ref[...] = (scores / denom).astype(BF16)
    mixed_all[head] = dot(weights_ref[...], v[...], (1, 0)).astype(BF16)

    def mixed_copy(j):
        return pltpu.make_async_remote_copy(
            src_ref=mixed_all.at[head],
            dst_ref=mixed_all.at[head],
            send_sem=mixed_send.at[j],
            recv_sem=mixed_recv.at[head],
            device_id=(peer(j), me),
            device_id_type=MESH,
        )

    def mixed_wait(j):
        pltpu.make_async_remote_copy(
            src_ref=mixed_all.at[peer(j)],
            dst_ref=mixed_all.at[peer(j)],
            send_sem=mixed_send.at[j],
            recv_sem=mixed_recv.at[peer(j)],
            device_id=(peer(j), me),
            device_id_type=MESH,
        ).wait_recv()

    each(heads - 1, lambda j: mixed_copy(j).start())

    on = on_ref[0].astype(F32)
    features = part.shape[1]
    flags = jnp.full((FLAG_ROWS, rows), 1.0, F32) * on
    body_rows = pl.ds(0, features)
    flag_rows = pl.ds(features, FLAG_ROWS)

    def order(i):
        if isinstance(i, int):
            return i // 2 if i % 2 == 0 else depth - 1 - i // 2
        return jnp.where(i % 2 == 0, i // 2, depth - 1 - i // 2)

    def core_copy(slot):
        return pltpu.make_async_remote_copy(
            core_out.at[slot], core_in.at[slot], core_out_sem.at[slot], core_in_sem.at[slot],
            device_id=sibling, device_id_type=MESH,
        )

    def x_copy(zz):
        return pltpu.make_async_remote_copy(
            x_out.at[zz], x_in.at[zz], x_out_sem.at[zz], x_in_sem.at[zz],
            device_id=across, device_id_type=MESH,
        )

    def z_copy(zz, source, other):
        return pltpu.make_async_remote_copy(
            z_out.at[zz], z_in.at[source], z_out_sem.at[zz], z_in_sem.at[source],
            device_id=line(other), device_id_type=MESH,
        )

    loads[3].wait()
    masked_t = dot(v[...], weights_ref[...], (0, 1)).astype(BF16) * on.astype(BF16)

    def sum_start(i):
        zz = order(i)
        at = pl.multiple_of(zz * group, group)
        product = dot(masked_t, cot[:, pl.ds(at, group)], (1, 0))
        for xx in (0, 1):
            slot = zz * 2 + xx
            first = product[:, 2 * xx * rows:(2 * xx + 1) * rows]
            second = product[:, (2 * xx + 1) * rows:(2 * xx + 2) * rows]
            part[slot] = jnp.where(c == 0, first, second)
            core_out[slot, body_rows] = jnp.where(c == 0, second, first).astype(BF16)
            core_out[slot, flag_rows] = flags.astype(BF16)
            core_copy(slot).start()

    def sum_x(i):
        zz = order(i)
        slot = zz * 2 + 1 - x
        core_copy(slot).wait_recv()
        x_out[zz, body_rows] = (
            part[slot] + core_in[slot, body_rows].astype(F32)
        ).astype(BF16)
        x_out[zz, flag_rows] = (flags + core_in[slot, flag_rows].astype(F32)).astype(BF16)
        x_copy(zz).start()

    def local_sum(zz):
        slot = zz * 2 + x
        core_copy(slot).wait_recv()
        x_copy(zz).wait_recv()
        main = (
            part[slot]
            + core_in[slot, body_rows].astype(F32)
            + x_in[zz, body_rows].astype(F32)
        )
        flag = (
            flags + core_in[slot, flag_rows].astype(F32) + x_in[zz, flag_rows].astype(F32)
        )
        return main, flag

    def sum_z(i):
        zz = order(i)

        @pl.when(zz != z)
        def _():
            main, flag = local_sum(zz)
            z_out[zz, body_rows] = main.astype(BF16)
            z_out[zz, flag_rows] = flag.astype(BF16)
            z_copy(zz, z, zz).start()

    def sum_end():
        main, flag = local_sum(z)
        total[body_rows] = main
        total[flag_rows] = flag

        def add(source):
            @pl.when(source != z)
            def _():
                z_copy(z, source, source).wait_recv()
                total[...] += z_in[source].astype(F32)

        each(depth, add)
        weight_grad_ref[...] = (total[body_rows] / total[pl.ds(features, 1)]).T

    def columns(zz):
        return pl.ds(pl.multiple_of(zz * group, group), group)

    def grad_group(d):
        def body(zz):
            core_wait(head, zz)
            mixed_grad[...] += dot(cot[:, columns(zz)], w_all[head, columns(zz)], (1, 0))

        around(d, body)

    def layer_copy(zz):
        return pltpu.make_async_copy(
            layer.at[:, columns(zz)], layer_hbm.at[0, :, columns(zz)], layer_sem.at[zz]
        )

    def term(hh, zz):
        return dot(mixed_all[hh], w_all[hh, columns(zz)], (1, 1)).astype(BF16).astype(F32)

    def layer_group(d):
        def body(zz):
            each(heads - 1, lambda j: core_wait(peer(j), zz))
            total = term(0, zz)
            if heads <= 4:
                for i in range(1, heads):
                    total = total + term(i, zz)
            else:
                total = lax.fori_loop(1, heads, lambda i, t: t + term(i, zz), total)
            layer[:, columns(zz)] = total.astype(BF16)
            layer_copy(zz).start()

        around(d, body)

    for d in range(2, depth):
        send_line(d)
    gather_z(1)
    for i in range(depth):
        sum_start(i)
        if i == 0:
            gather_x(0)
        if i > 0:
            sum_x(i - 1)
    sum_x(depth - 1)
    mixed_grad[...] = jnp.zeros_like(mixed_grad)
    for d in range(2, depth):
        gather_z(d)
        sum_z(d - 2)
        gather_x(d - 1)
    sum_z(depth - 2)
    sum_z(depth - 1)
    each(heads - 1, mixed_wait)
    for i in range(depth):
        gather_heads(i)
        grad_group(i)
        if i == 0:
            gather_x(depth - 1)
        if i < depth - 1:
            layer_group(i)
    value_grad_ref[0] = dot(
        weights_ref[...], mixed_grad[...].astype(BF16), (0, 0)
    ).astype(BF16)
    sum_end()
    layer_group(depth - 1)

    each(depth, lambda i: layer_copy(i).wait())
    each(heads - 1, lambda j: mixed_copy(j).wait_send())

    def drain(zz):
        rr = rep(zz, x, c)
        far = rep(zz, 1 - x, c)

        def one(hh):
            to_core(hh, rr).wait_send()
            to_core(hh, far).wait_send()

        each(heads, one)
        each(heads - 1, lambda j: to_peer(j, rr).wait_send())
        each(heads - 1, lambda j: to_peer(j, far).wait_send())
        to_across(rr).wait_send()
        core_copy(zz * 2).wait_send()
        core_copy(zz * 2 + 1).wait_send()
        x_copy(zz).wait_send()

        @pl.when(zz != z)
        def _():
            to_line(zz).wait_send()
            z_copy(zz, z, zz).wait_send()

    each(depth, drain)


def hand_over(pieces, *refs):
    load_sem, store_sem = refs[-2:]
    moves = []
    for src, dst, held in zip(refs[:3], refs[3:6], refs[6:9]):
        count = pieces if src.shape[-2] * src.shape[-1] > 65536 * pieces else 1
        step = src.shape[-2] // count
        for i in range(count):
            cut = (0,) * (len(src.shape) - 2) + (pl.ds(i * step, step),)
            n = len(moves)
            moves.append((
                pltpu.make_async_copy(src.at[cut], held.at[cut], load_sem.at[n]),
                pltpu.make_async_copy(held.at[cut], dst.at[cut], store_sem.at[n]),
            ))
    for load, _ in moves:
        load.start()
    for load, store in moves:
        load.wait()
        store.start()
    for _, store in moves:
        store.wait()


def local(heads, replicas, queries, keys, values, out_weight, cotangent, on_time):
    _, tokens, features = queries.shape
    value_features = values.shape[2]
    rows = out_weight.shape[0]
    model = cotangent.shape[2]
    depth = replicas // 4
    summed = (value_features + FLAG_ROWS, rows)
    hbm = pl.BlockSpec(memory_space=pltpu.HBM)
    vmem = pl.BlockSpec(memory_space=pltpu.VMEM)
    dma = pltpu.SemaphoreType.DMA
    outputs = pl.pallas_call(
        functools.partial(kernel, heads, replicas),
        out_shape=(
            jax.ShapeDtypeStruct(cotangent.shape, BF16),
            jax.ShapeDtypeStruct(values.shape, BF16),
            jax.ShapeDtypeStruct(out_weight.shape, F32),
        ),
        in_specs=[hbm] * 5 + [pl.BlockSpec(memory_space=pltpu.SMEM)],
        out_specs=(hbm, vmem, vmem),
        scratch_shapes=[
            pltpu.VMEM((tokens, features), BF16),
            pltpu.VMEM((tokens, features), BF16),
            pltpu.VMEM((tokens, value_features), BF16),
            pltpu.VMEM((tokens, model), BF16),
            pltpu.VMEM((tokens, model), BF16),
            pltpu.VMEM((heads, model, value_features), BF16),
            pltpu.VMEM((heads, tokens, value_features), BF16),
            pltpu.VMEM((tokens, value_features), F32),
            pltpu.VMEM((depth * 2, value_features, rows), F32),
            pltpu.VMEM(summed, F32),
            pltpu.VMEM((tokens, tokens), BF16),
            pltpu.VMEM((depth * 2,) + summed, BF16),
            pltpu.VMEM((depth * 2,) + summed, BF16),
            pltpu.VMEM((depth,) + summed, BF16),
            pltpu.VMEM((depth,) + summed, BF16),
            pltpu.VMEM((depth,) + summed, BF16),
            pltpu.VMEM((depth,) + summed, BF16),
            dma((5,)),
            dma((depth,)),
            dma((heads, replicas)),
            dma((depth,)),
            dma((replicas,)),
            dma((heads, replicas)),
            dma((heads, replicas)),
            dma((heads,)),
            dma((heads,)),
            dma((depth * 2,)),
            dma((depth * 2,)),
            dma((depth,)),
            dma((depth,)),
            dma((depth,)),
            dma((depth,)),
        ],
        compiler_params=pltpu.CompilerParams(
            collective_id=0, has_side_effects=True, vmem_limit_bytes=56 * 1024 * 1024
        ),
    )(queries, keys, values, out_weight, cotangent, on_time)
    return pl.pallas_call(
        functools.partial(hand_over, 8),
        out_shape=tuple(jax.ShapeDtypeStruct(o.shape, o.dtype) for o in outputs),
        in_specs=[hbm] * 3,
        out_specs=(hbm,) * 3,
        scratch_shapes=[pltpu.VMEM(o.shape, o.dtype) for o in outputs] + [dma((10,)), dma((10,))],
        compiler_params=pltpu.CompilerParams(vmem_limit_bytes=56 * 1024 * 1024),
    )(*outputs)


def solution(mesh):
    return jax.shard_map(
        functools.partial(local, mesh.shape["head"], mesh.shape["replica"]),
        mesh=mesh,
        in_specs=(
            P("replica", None, "head"),
            P("replica", None, "head"),
            P("replica", None, "head"),
            P("replica", "head"),
            P("replica", None, None),
            P("replica"),
        ),
        out_specs=(P("replica", None, None), P("replica", None, "head"), P("replica", "head")),
        check_vma=False,
    )
```

```python
import functools
import math

import jax
import jax.numpy as jnp
from jax import lax
from jax.experimental import pallas as pl
from jax.experimental.pallas import tpu as pltpu
from jax.sharding import PartitionSpec as P

MESH = pl.DeviceIdType.MESH
FLAG_ROWS = 16
F32 = jnp.float32
BF16 = jnp.bfloat16


def dot(a, b, dims):
    return lax.dot_general(a, b, ((dims[:1], dims[1:]), ((), ())), preferred_element_type=F32)


def each(count, body):
    if count <= 4:
        for i in range(count):
            body(i)
    else:
        lax.fori_loop(0, count, lambda i, c: (body(i), c)[1], 0)


def when(cond, body):
    if isinstance(cond, bool):
        if cond:
            body()
    else:
        pl.when(cond)(body)


def kernel(
    heads, replicas,
    q_hbm, k_hbm, v_hbm, w_hbm, cot_hbm, on_ref,
    layer_hbm, value_grad_ref, weight_grad_ref,
    q, k, v, cot, layer, w_all, mixed_all, mixed_grad, part, total, weights_ref,
    core_out, core_in, x_out, x_in, z_out, z_in,
    load_sem, layer_sem,
    w_recv, up_send, down_send, partner_send, x_send, head_send, core_send,
    mixed_send, mixed_recv,
    core_out_sem, core_in_sem, x_out_sem, x_in_sem, z_out_sem, z_in_sem,
):
    depth = replicas // 4
    rows = w_hbm.shape[0]
    group = 4 * rows
    tokens = q.shape[0]
    head = lax.axis_index("head")
    me = lax.axis_index("replica")
    z, x, c = me // 4, (me // 2) % 2, me % 2

    def rep(zz, xx, cc):
        return zz * 4 + xx * 2 + cc

    sibling = (head, rep(z, x, 1 - c))
    across = (head, rep(z, 1 - x, c))

    def line(zz):
        return (head, rep(zz, x, c))

    def peer(j):
        return lax.rem(head + 1 + j, heads)

    barrier = pltpu.get_barrier_semaphore()

    def greet(device):
        pl.semaphore_signal(barrier, inc=1, device_id=device, device_id_type=MESH)

    greet(sibling)
    greet(across)
    each(heads - 1, lambda j: greet((peer(j), me)))
    each(depth, lambda zz: pl.when(zz != z)(lambda: greet(line(zz))))

    loads = [
        pltpu.make_async_copy(src, dst, load_sem.at[i])
        for i, (src, dst) in enumerate(
            ((q_hbm.at[0], q), (k_hbm.at[0], k), (v_hbm.at[0], v), (cot_hbm.at[0], cot),
             (w_hbm, w_all.at[head, pl.ds(pl.multiple_of(me * rows, rows), rows)]))
        )
    ]
    for load in loads:
        load.start()
    pl.semaphore_wait(barrier, heads + depth)

    def block(hh, rr):
        return w_all.at[hh, pl.ds(pl.multiple_of(rr * rows, rows), rows)]

    def w_copy(hh, rr, sem, device):
        return pltpu.make_async_remote_copy(
            src_ref=block(hh, rr),
            dst_ref=block(hh, rr),
            send_sem=sem,
            recv_sem=w_recv.at[hh, rr],
            device_id=device,
            device_id_type=MESH,
        )

    def w_wait(hh, rr):
        w_copy(hh, rr, core_send.at[hh, rr], sibling).wait_recv()

    def to_above(rr):
        return w_copy(head, rr, up_send.at[rr], line(z + 1))

    def to_below(rr):
        return w_copy(head, rr, down_send.at[rr], line(z - 1))

    def to_partner(hh, rr):
        return w_copy(hh, rr, partner_send.at[hh, rr], line(z + 1 - 2 * (z % 2)))

    def to_across(rr):
        return w_copy(head, rr, x_send.at[rr], across)

    def to_peer(j, rr):
        return w_copy(head, rr, head_send.at[j, rr], (peer(j), me))

    def to_core(hh, rr):
        return w_copy(hh, rr, core_send.at[hh, rr], sibling)

    def to_peers(rr):
        each(heads - 1, lambda j: to_peer(j, rr).start())

    def around(d, body):
        if isinstance(d, int) and d == 0:
            body(z)
        else:
            pl.when(z - d >= 0)(lambda: body(z - d))
            pl.when(z + d < depth)(lambda: body(z + d))

    loads[4].wait()
    pl.when(z < depth - 1)(lambda: to_above(me).start())
    pl.when(z > 0)(lambda: to_below(me).start())
    to_peers(me)
    to_across(me).start()
    to_core(head, me).start()

    def gather_z(d):
        def body(zz):
            rr = rep(zz, x, c)
            w_wait(head, rr)
            pl.when((zz < z) & (z < depth - 1))(lambda: to_above(rr).start())
            pl.when((zz > z) & (z > 0))(lambda: to_below(rr).start())
            if d % 2 == 0:
                to_peers(rr)
            to_across(rr).start()
            to_core(head, rr).start()

        around(d, body)

    def gather_x(d):
        def body(zz):
            rr = rep(zz, 1 - x, c)
            w_wait(head, rr)
            to_peers(rr)
            to_core(head, rr).start()

        around(d, body)

    def gather_y(d):
        def body(zz):
            def from_peer(j):
                rr = rep(zz, x, c)
                w_wait(peer(j), rr)
                to_partner(peer(j), rr).start()
                to_core(peer(j), rr).start()

            each(heads - 1, from_peer)

        around(d, body)

    def gather_heads(d):
        def body(zz):
            def from_peer(j):
                for xx in (x, 1 - x) if d % 2 else (1 - x,):
                    w_wait(peer(j), rep(zz, xx, c))
                    to_core(peer(j), rep(zz, xx, c)).start()

            each(heads - 1, from_peer)

        around(d, body)

    def core_wait(hh, zz):
        for xx in (0, 1):
            w_wait(hh, rep(zz, xx, 1 - c))

    for load in loads[:3]:
        load.wait()
    row = lax.broadcasted_iota(jnp.int32, (tokens, tokens), 0)
    col = lax.broadcasted_iota(jnp.int32, (tokens, tokens), 1)
    offset = (row - col).astype(F32)
    log_gamma = jnp.float32(math.log(1.0 - 2.0 ** -5.0))
    for i in range(1, heads):
        log_gamma = jnp.where(head == i, jnp.float32(math.log(1.0 - 2.0 ** (-5.0 - i))), log_gamma)
    decay = jnp.where(offset >= 0.0, jnp.exp(jnp.maximum(offset, 0.0) * log_gamma), 0.0)
    scores = dot(q[...], k[...], (1, 1)) * decay
    denom = jnp.maximum(jnp.sum(jnp.abs(scores), axis=-1, keepdims=True), 1.0)
    weights_ref[...] = (scores / denom).astype(BF16)
    mixed_all[head] = dot(weights_ref[...], v[...], (1, 0)).astype(BF16)

    def mixed_copy(j):
        return pltpu.make_async_remote_copy(
            src_ref=mixed_all.at[head],
            dst_ref=mixed_all.at[head],
            send_sem=mixed_send.at[j],
            recv_sem=mixed_recv.at[head],
            device_id=(peer(j), me),
            device_id_type=MESH,
        )

    def mixed_wait(j):
        pltpu.make_async_remote_copy(
            src_ref=mixed_all.at[peer(j)],
            dst_ref=mixed_all.at[peer(j)],
            send_sem=mixed_send.at[j],
            recv_sem=mixed_recv.at[peer(j)],
            device_id=(peer(j), me),
            device_id_type=MESH,
        ).wait_recv()

    each(heads - 1, lambda j: mixed_copy(j).start())

    on = on_ref[0].astype(F32)
    features = part.shape[1]
    flags = jnp.full((FLAG_ROWS, rows), 1.0, F32) * on
    body_rows = pl.ds(0, features)
    flag_rows = pl.ds(features, FLAG_ROWS)

    def order(i):
        if isinstance(i, int):
            return i // 2 if i % 2 == 0 else depth - 1 - i // 2
        return jnp.where(i % 2 == 0, i // 2, depth - 1 - i // 2)

    def core_copy(slot):
        return pltpu.make_async_remote_copy(
            core_out.at[slot], core_in.at[slot], core_out_sem.at[slot], core_in_sem.at[slot],
            device_id=sibling, device_id_type=MESH,
        )

    def x_copy(zz):
        return pltpu.make_async_remote_copy(
            x_out.at[zz], x_in.at[zz], x_out_sem.at[zz], x_in_sem.at[zz],
            device_id=across, device_id_type=MESH,
        )

    def z_copy(zz, source, other):
        return pltpu.make_async_remote_copy(
            z_out.at[zz], z_in.at[source], z_out_sem.at[zz], z_in_sem.at[source],
            device_id=line(other), device_id_type=MESH,
        )

    loads[3].wait()
    masked_t = dot(v[...], weights_ref[...], (0, 1)).astype(BF16) * on.astype(BF16)

    def sum_start(i):
        zz = order(i)
        at = pl.multiple_of(zz * group, group)
        product = dot(masked_t, cot[:, pl.ds(at, group)], (1, 0))
        for xx in (0, 1):
            slot = zz * 2 + xx
            first = product[:, 2 * xx * rows:(2 * xx + 1) * rows]
            second = product[:, (2 * xx + 1) * rows:(2 * xx + 2) * rows]
            part[slot] = jnp.where(c == 0, first, second)
            core_out[slot, body_rows] = jnp.where(c == 0, second, first).astype(BF16)
            core_out[slot, flag_rows] = flags.astype(BF16)
            core_copy(slot).start()

    def sum_x(i):
        zz = order(i)
        slot = zz * 2 + 1 - x
        core_copy(slot).wait_recv()
        x_out[zz, body_rows] = (
            part[slot] + core_in[slot, body_rows].astype(F32)
        ).astype(BF16)
        x_out[zz, flag_rows] = (flags + core_in[slot, flag_rows].astype(F32)).astype(BF16)
        x_copy(zz).start()

    def local_sum(zz):
        slot = zz * 2 + x
        core_copy(slot).wait_recv()
        x_copy(zz).wait_recv()
        main = (
            part[slot]
            + core_in[slot, body_rows].astype(F32)
            + x_in[zz, body_rows].astype(F32)
        )
        flag = (
            flags + core_in[slot, flag_rows].astype(F32) + x_in[zz, flag_rows].astype(F32)
        )
        return main, flag

    def sum_z(i):
        zz = order(i)

        @pl.when(zz != z)
        def _():
            main, flag = local_sum(zz)
            z_out[zz, body_rows] = main.astype(BF16)
            z_out[zz, flag_rows] = flag.astype(BF16)
            z_copy(zz, z, zz).start()

    def sum_end():
        main, flag = local_sum(z)
        total[body_rows] = main
        total[flag_rows] = flag

        def add(source):
            @pl.when(source != z)
            def _():
                z_copy(z, source, source).wait_recv()
                total[...] += z_in[source].astype(F32)

        each(depth, add)
        weight_grad_ref[...] = (total[body_rows] / total[pl.ds(features, 1)]).T

    def columns(zz):
        return pl.ds(pl.multiple_of(zz * group, group), group)

    def grad_group(d):
        def body(zz):
            core_wait(head, zz)
            mixed_grad[...] += dot(cot[:, columns(zz)], w_all[head, columns(zz)], (1, 0))

        around(d, body)

    def layer_copy(zz):
        return pltpu.make_async_copy(
            layer.at[:, columns(zz)], layer_hbm.at[0, :, columns(zz)], layer_sem.at[zz]
        )

    def term(hh, zz):
        return dot(mixed_all[hh], w_all[hh, columns(zz)], (1, 1)).astype(BF16).astype(F32)

    def layer_group(d):
        def body(zz):
            each(heads - 1, lambda j: core_wait(peer(j), zz))
            total = term(0, zz)
            if heads <= 4:
                for i in range(1, heads):
                    total = total + term(i, zz)
            else:
                total = lax.fori_loop(1, heads, lambda i, t: t + term(i, zz), total)
            layer[:, columns(zz)] = total.astype(BF16)
            layer_copy(zz).start()

        around(d, body)

    gather_z(1)
    for i in range(depth):
        sum_start(i)
        if i == 0:
            gather_x(0)
            gather_y(0)
        if i > 0:
            sum_x(i - 1)
    sum_x(depth - 1)
    mixed_grad[...] = jnp.zeros_like(mixed_grad)
    for d in range(2, depth):
        gather_z(d)
        sum_z(d - 2)
        gather_x(d - 1)
        if d % 2:
            gather_y(d - 1)
    sum_z(depth - 2)
    sum_z(depth - 1)
    each(heads - 1, mixed_wait)
    for i in range(depth):
        gather_heads(i)
        grad_group(i)
        if i == 0:
            gather_x(depth - 1)
        if i < depth - 1:
            layer_group(i)
    value_grad_ref[0] = dot(
        weights_ref[...], mixed_grad[...].astype(BF16), (0, 0)
    ).astype(BF16)
    sum_end()
    layer_group(depth - 1)

    each(depth, lambda i: layer_copy(i).wait())
    each(heads - 1, lambda j: mixed_copy(j).wait_send())

    def drain(zz):
        rr = rep(zz, x, c)
        far = rep(zz, 1 - x, c)

        def one(hh):
            to_core(hh, rr).wait_send()
            to_core(hh, far).wait_send()

        each(heads, one)
        each(heads - 1, lambda j: to_peer(j, far).wait_send())

        @pl.when((zz + z) % 2 == 0)
        def _():
            def shared(j):
                to_peer(j, rr).wait_send()
                to_partner(peer(j), rr).wait_send()

            each(heads - 1, shared)

        pl.when((zz <= z) & (z < depth - 1))(lambda: to_above(rr).wait_send())
        pl.when((zz >= z) & (z > 0))(lambda: to_below(rr).wait_send())
        to_across(rr).wait_send()
        core_copy(zz * 2).wait_send()
        core_copy(zz * 2 + 1).wait_send()
        x_copy(zz).wait_send()

        @pl.when(zz != z)
        def _():
            z_copy(zz, z, zz).wait_send()

    each(depth, drain)


def hand_over(pieces, *refs):
    load_sem, store_sem = refs[-2:]
    moves = []
    for src, dst, held in zip(refs[:3], refs[3:6], refs[6:9]):
        count = pieces if src.shape[-2] * src.shape[-1] > 65536 * pieces else 1
        step = src.shape[-2] // count
        for i in range(count):
            cut = (0,) * (len(src.shape) - 2) + (pl.ds(i * step, step),)
            n = len(moves)
            moves.append((
                pltpu.make_async_copy(src.at[cut], held.at[cut], load_sem.at[n]),
                pltpu.make_async_copy(held.at[cut], dst.at[cut], store_sem.at[n]),
            ))
    for load, _ in moves:
        load.start()
    for load, store in moves:
        load.wait()
        store.start()
    for _, store in moves:
        store.wait()


def local(heads, replicas, queries, keys, values, out_weight, cotangent, on_time):
    _, tokens, features = queries.shape
    value_features = values.shape[2]
    rows = out_weight.shape[0]
    model = cotangent.shape[2]
    depth = replicas // 4
    summed = (value_features + FLAG_ROWS, rows)
    hbm = pl.BlockSpec(memory_space=pltpu.HBM)
    vmem = pl.BlockSpec(memory_space=pltpu.VMEM)
    dma = pltpu.SemaphoreType.DMA
    outputs = pl.pallas_call(
        functools.partial(kernel, heads, replicas),
        out_shape=(
            jax.ShapeDtypeStruct(cotangent.shape, BF16),
            jax.ShapeDtypeStruct(values.shape, BF16),
            jax.ShapeDtypeStruct(out_weight.shape, F32),
        ),
        in_specs=[hbm] * 5 + [pl.BlockSpec(memory_space=pltpu.SMEM)],
        out_specs=(hbm, vmem, vmem),
        scratch_shapes=[
            pltpu.VMEM((tokens, features), BF16),
            pltpu.VMEM((tokens, features), BF16),
            pltpu.VMEM((tokens, value_features), BF16),
            pltpu.VMEM((tokens, model), BF16),
            pltpu.VMEM((tokens, model), BF16),
            pltpu.VMEM((heads, model, value_features), BF16),
            pltpu.VMEM((heads, tokens, value_features), BF16),
            pltpu.VMEM((tokens, value_features), F32),
            pltpu.VMEM((depth * 2, value_features, rows), F32),
            pltpu.VMEM(summed, F32),
            pltpu.VMEM((tokens, tokens), BF16),
            pltpu.VMEM((depth * 2,) + summed, BF16),
            pltpu.VMEM((depth * 2,) + summed, BF16),
            pltpu.VMEM((depth,) + summed, BF16),
            pltpu.VMEM((depth,) + summed, BF16),
            pltpu.VMEM((depth,) + summed, BF16),
            pltpu.VMEM((depth,) + summed, BF16),
            dma((5,)),
            dma((depth,)),
            dma((heads, replicas)),
            dma((replicas,)),
            dma((replicas,)),
            dma((heads, replicas)),
            dma((replicas,)),
            dma((heads, replicas)),
            dma((heads, replicas)),
            dma((heads,)),
            dma((heads,)),
            dma((depth * 2,)),
            dma((depth * 2,)),
            dma((depth,)),
            dma((depth,)),
            dma((depth,)),
            dma((depth,)),
        ],
        compiler_params=pltpu.CompilerParams(
            collective_id=0, has_side_effects=True, vmem_limit_bytes=56 * 1024 * 1024
        ),
    )(queries, keys, values, out_weight, cotangent, on_time)
    return pl.pallas_call(
        functools.partial(hand_over, 8),
        out_shape=tuple(jax.ShapeDtypeStruct(o.shape, o.dtype) for o in outputs),
        in_specs=[hbm] * 3,
        out_specs=(hbm,) * 3,
        scratch_shapes=[pltpu.VMEM(o.shape, o.dtype) for o in outputs] + [dma((10,)), dma((10,))],
        compiler_params=pltpu.CompilerParams(vmem_limit_bytes=56 * 1024 * 1024),
    )(*outputs)


def solution(mesh):
    return jax.shard_map(
        functools.partial(local, mesh.shape["head"], mesh.shape["replica"]),
        mesh=mesh,
        in_specs=(
            P("replica", None, "head"),
            P("replica", None, "head"),
            P("replica", None, "head"),
            P("replica", "head"),
            P("replica", None, None),
            P("replica"),
        ),
        out_specs=(P("replica", None, None), P("replica", None, "head"), P("replica", "head")),
        check_vma=False,
    )
```

```python
import functools
import math

import jax
import jax.numpy as jnp
from jax import lax
from jax.experimental import pallas as pl
from jax.experimental.pallas import tpu as pltpu
from jax.sharding import PartitionSpec as P

MESH = pl.DeviceIdType.MESH
FLAG_ROWS = 16
F32 = jnp.float32
BF16 = jnp.bfloat16


def dot(a, b, dims):
    return lax.dot_general(a, b, ((dims[:1], dims[1:]), ((), ())), preferred_element_type=F32)


def each(count, body):
    if count <= 4:
        for i in range(count):
            body(i)
    else:
        lax.fori_loop(0, count, lambda i, c: (body(i), c)[1], 0)


def when(cond, body):
    if isinstance(cond, bool):
        if cond:
            body()
    else:
        pl.when(cond)(body)


def kernel(
    heads, replicas,
    q_hbm, k_hbm, v_hbm, w_hbm, cot_hbm, on_ref,
    layer_hbm, value_grad_ref, weight_grad_ref,
    q, k, v, cot, layer, w_all, mixed_all, mixed_grad, part, total, weights_ref,
    core_out, core_in, x_out, x_in, z_out, z_in,
    load_sem, layer_sem,
    w_recv, up_send, down_send, partner_send, x_send, head_send, core_send,
    mixed_send, mixed_recv,
    core_out_sem, core_in_sem, x_out_sem, x_in_sem, z_out_sem, z_in_sem,
):
    depth = replicas // 4
    rows = w_hbm.shape[0]
    group = 4 * rows
    tokens = q.shape[0]
    head = lax.axis_index("head")
    me = lax.axis_index("replica")
    z, x, c = me // 4, (me // 2) % 2, me % 2

    def rep(zz, xx, cc):
        return zz * 4 + xx * 2 + cc

    sibling = (head, rep(z, x, 1 - c))
    across = (head, rep(z, 1 - x, c))

    def line(zz):
        return (head, rep(zz, x, c))

    def peer(j):
        return lax.rem(head + 1 + j, heads)

    barrier = pltpu.get_barrier_semaphore()

    def greet(device):
        pl.semaphore_signal(barrier, inc=1, device_id=device, device_id_type=MESH)

    greet(sibling)
    greet(across)
    each(heads - 1, lambda j: greet((peer(j), me)))
    each(depth, lambda zz: pl.when(zz != z)(lambda: greet(line(zz))))

    loads = [
        pltpu.make_async_copy(src, dst, load_sem.at[i])
        for i, (src, dst) in enumerate(
            ((q_hbm.at[0], q), (k_hbm.at[0], k), (v_hbm.at[0], v), (cot_hbm.at[0], cot),
             (w_hbm, w_all.at[head, pl.ds(pl.multiple_of(me * rows, rows), rows)]))
        )
    ]
    for load in loads:
        load.start()
    pl.semaphore_wait(barrier, heads + depth)

    def block(hh, rr):
        return w_all.at[hh, pl.ds(pl.multiple_of(rr * rows, rows), rows)]

    def w_copy(hh, rr, sem, device):
        return pltpu.make_async_remote_copy(
            src_ref=block(hh, rr),
            dst_ref=block(hh, rr),
            send_sem=sem,
            recv_sem=w_recv.at[hh, rr],
            device_id=device,
            device_id_type=MESH,
        )

    def w_wait(hh, rr):
        w_copy(hh, rr, core_send.at[hh, rr], sibling).wait_recv()

    def to_above(rr):
        return w_copy(head, rr, up_send.at[rr], line(z + 1))

    def to_below(rr):
        return w_copy(head, rr, down_send.at[rr], line(z - 1))

    def to_partner(hh, rr):
        return w_copy(hh, rr, partner_send.at[hh, rr], line(z + 1 - 2 * (z % 2)))

    def to_across(rr):
        return w_copy(head, rr, x_send.at[rr], across)

    def to_peer(j, rr):
        return w_copy(head, rr, head_send.at[j, rr], (peer(j), me))

    def to_core(hh, rr):
        return w_copy(hh, rr, core_send.at[hh, rr], sibling)

    def to_peers(rr):
        each(heads - 1, lambda j: to_peer(j, rr).start())

    def around(d, body):
        if isinstance(d, int) and d == 0:
            body(z)
        else:
            pl.when(z - d >= 0)(lambda: body(z - d))
            pl.when(z + d < depth)(lambda: body(z + d))

    loads[4].wait()
    pl.when(z < depth - 1)(lambda: to_above(me).start())
    pl.when(z > 0)(lambda: to_below(me).start())
    to_peers(me)
    to_across(me).start()
    to_core(head, me).start()

    def gather_z(d):
        def body(zz):
            rr = rep(zz, x, c)
            w_wait(head, rr)
            pl.when((zz < z) & (z < depth - 1))(lambda: to_above(rr).start())
            pl.when((zz > z) & (z > 0))(lambda: to_below(rr).start())
            if d % 2 == 0:
                to_peers(rr)
            to_across(rr).start()
            to_core(head, rr).start()

        around(d, body)

    def gather_x(d):
        def body(zz):
            rr = rep(zz, 1 - x, c)
            w_wait(head, rr)
            to_peers(rr)
            to_core(head, rr).start()

        around(d, body)

    def gather_y(d):
        def body(zz):
            def from_peer(j):
                rr = rep(zz, x, c)
                w_wait(peer(j), rr)
                to_partner(peer(j), rr).start()
                to_core(peer(j), rr).start()

            each(heads - 1, from_peer)

        around(d, body)

    def gather_heads(d):
        def body(zz):
            def from_peer(j):
                for xx in (x, 1 - x) if d % 2 else (1 - x,):
                    w_wait(peer(j), rep(zz, xx, c))
                    to_core(peer(j), rep(zz, xx, c)).start()

            each(heads - 1, from_peer)

        around(d, body)

    def core_wait(hh, zz):
        for xx in (0, 1):
            w_wait(hh, rep(zz, xx, 1 - c))

    for load in loads[:3]:
        load.wait()
    row = lax.broadcasted_iota(jnp.int32, (tokens, tokens), 0)
    col = lax.broadcasted_iota(jnp.int32, (tokens, tokens), 1)
    offset = (row - col).astype(F32)
    log_gamma = jnp.float32(math.log(1.0 - 2.0 ** -5.0))
    for i in range(1, heads):
        log_gamma = jnp.where(head == i, jnp.float32(math.log(1.0 - 2.0 ** (-5.0 - i))), log_gamma)
    decay = jnp.where(offset >= 0.0, jnp.exp(jnp.maximum(offset, 0.0) * log_gamma), 0.0)
    scores = dot(q[...], k[...], (1, 1)) * decay
    denom = jnp.maximum(jnp.sum(jnp.abs(scores), axis=-1, keepdims=True), 1.0)
    weights_ref[...] = (scores / denom).astype(BF16)
    mixed_all[head] = dot(weights_ref[...], v[...], (1, 0)).astype(BF16)

    def mixed_copy(j):
        return pltpu.make_async_remote_copy(
            src_ref=mixed_all.at[head],
            dst_ref=mixed_all.at[head],
            send_sem=mixed_send.at[j],
            recv_sem=mixed_recv.at[head],
            device_id=(peer(j), me),
            device_id_type=MESH,
        )

    def mixed_wait(j):
        pltpu.make_async_remote_copy(
            src_ref=mixed_all.at[peer(j)],
            dst_ref=mixed_all.at[peer(j)],
            send_sem=mixed_send.at[j],
            recv_sem=mixed_recv.at[peer(j)],
            device_id=(peer(j), me),
            device_id_type=MESH,
        ).wait_recv()

    each(heads - 1, lambda j: mixed_copy(j).start())

    on = on_ref[0].astype(F32)
    features = part.shape[1]
    flags = jnp.full((FLAG_ROWS, rows), 1.0, F32) * on
    body_rows = pl.ds(0, features)
    flag_rows = pl.ds(features, FLAG_ROWS)

    def order(i):
        if isinstance(i, int):
            return i // 2 if i % 2 == 0 else depth - 1 - i // 2
        return jnp.where(i % 2 == 0, i // 2, depth - 1 - i // 2)

    def core_copy(slot):
        return pltpu.make_async_remote_copy(
            core_out.at[slot], core_in.at[slot], core_out_sem.at[slot], core_in_sem.at[slot],
            device_id=sibling, device_id_type=MESH,
        )

    def x_copy(zz):
        return pltpu.make_async_remote_copy(
            x_out.at[zz], x_in.at[zz], x_out_sem.at[zz], x_in_sem.at[zz],
            device_id=across, device_id_type=MESH,
        )

    def z_copy(zz, source, other):
        return pltpu.make_async_remote_copy(
            z_out.at[zz], z_in.at[source], z_out_sem.at[zz], z_in_sem.at[source],
            device_id=line(other), device_id_type=MESH,
        )

    loads[3].wait()
    masked_t = dot(v[...], weights_ref[...], (0, 1)).astype(BF16) * on.astype(BF16)

    def sum_start(i):
        zz = order(i)
        at = pl.multiple_of(zz * group, group)
        product = dot(masked_t, cot[:, pl.ds(at, group)], (1, 0))
        for xx in (0, 1):
            slot = zz * 2 + xx
            first = product[:, 2 * xx * rows:(2 * xx + 1) * rows]
            second = product[:, (2 * xx + 1) * rows:(2 * xx + 2) * rows]
            part[slot] = jnp.where(c == 0, first, second)
            core_out[slot, body_rows] = jnp.where(c == 0, second, first).astype(BF16)
            core_out[slot, flag_rows] = flags.astype(BF16)
            core_copy(slot).start()

    def sum_x(i):
        zz = order(i)
        slot = zz * 2 + 1 - x
        core_copy(slot).wait_recv()
        x_out[zz, body_rows] = (
            part[slot] + core_in[slot, body_rows].astype(F32)
        ).astype(BF16)
        x_out[zz, flag_rows] = (flags + core_in[slot, flag_rows].astype(F32)).astype(BF16)
        x_copy(zz).start()

    def local_sum(zz):
        slot = zz * 2 + x
        core_copy(slot).wait_recv()
        x_copy(zz).wait_recv()
        main = (
            part[slot]
            + core_in[slot, body_rows].astype(F32)
            + x_in[zz, body_rows].astype(F32)
        )
        flag = (
            flags + core_in[slot, flag_rows].astype(F32) + x_in[zz, flag_rows].astype(F32)
        )
        return main, flag

    def sum_z(i):
        zz = order(i)

        @pl.when(zz != z)
        def _():
            main, flag = local_sum(zz)
            z_out[zz, body_rows] = main.astype(BF16)
            z_out[zz, flag_rows] = flag.astype(BF16)
            z_copy(zz, z, zz).start()

    def sum_end():
        main, flag = local_sum(z)
        total[body_rows] = main
        total[flag_rows] = flag

        def add(source):
            @pl.when(source != z)
            def _():
                z_copy(z, source, source).wait_recv()
                total[...] += z_in[source].astype(F32)

        each(depth, add)
        weight_grad_ref[...] = (total[body_rows] / total[pl.ds(features, 1)]).T

    def columns(zz):
        return pl.ds(pl.multiple_of(zz * group, group), group)

    def grad_group(d):
        def body(zz):
            core_wait(head, zz)
            mixed_grad[...] += dot(cot[:, columns(zz)], w_all[head, columns(zz)], (1, 0))

        around(d, body)

    def layer_copy(zz):
        return pltpu.make_async_copy(
            layer.at[:, columns(zz)], layer_hbm.at[0, :, columns(zz)], layer_sem.at[zz]
        )

    def term(hh, zz):
        return dot(mixed_all[hh], w_all[hh, columns(zz)], (1, 1)).astype(BF16).astype(F32)

    def layer_group(d):
        def body(zz):
            each(heads - 1, lambda j: core_wait(peer(j), zz))
            total = term(0, zz)
            if heads <= 4:
                for i in range(1, heads):
                    total = total + term(i, zz)
            else:
                total = lax.fori_loop(1, heads, lambda i, t: t + term(i, zz), total)
            layer[:, columns(zz)] = total.astype(BF16)
            layer_copy(zz).start()

        around(d, body)

    gather_z(1)
    for i in range(depth):
        sum_start(i)
        if i == 0:
            gather_x(0)
            gather_y(0)
        if i > 0:
            sum_x(i - 1)
    sum_x(depth - 1)
    mixed_grad[...] = jnp.zeros_like(mixed_grad)
    for d in range(2, depth):
        gather_z(d)
        if d < depth - 1:
            gather_x(d - 1)
        sum_z(d - 2)
        if d % 2:
            gather_y(d - 1)
    sum_z(depth - 2)
    sum_z(depth - 1)
    gather_x(depth - 2)
    each(heads - 1, mixed_wait)
    for i in range(depth - 1):
        gather_heads(i)
        grad_group(i)
        if i == 0:
            gather_x(depth - 1)
        layer_group(i)
    grad_group(depth - 1)
    value_grad_ref[0] = dot(
        weights_ref[...], mixed_grad[...].astype(BF16), (0, 0)
    ).astype(BF16)
    gather_heads(depth - 1)
    sum_end()
    layer_group(depth - 1)

    each(depth, lambda i: layer_copy(i).wait())
    each(heads - 1, lambda j: mixed_copy(j).wait_send())

    def drain(zz):
        rr = rep(zz, x, c)
        far = rep(zz, 1 - x, c)

        def one(hh):
            to_core(hh, rr).wait_send()
            to_core(hh, far).wait_send()

        each(heads, one)
        each(heads - 1, lambda j: to_peer(j, far).wait_send())

        @pl.when((zz + z) % 2 == 0)
        def _():
            def shared(j):
                to_peer(j, rr).wait_send()
                to_partner(peer(j), rr).wait_send()

            each(heads - 1, shared)

        pl.when((zz <= z) & (z < depth - 1))(lambda: to_above(rr).wait_send())
        pl.when((zz >= z) & (z > 0))(lambda: to_below(rr).wait_send())
        to_across(rr).wait_send()
        core_copy(zz * 2).wait_send()
        core_copy(zz * 2 + 1).wait_send()
        x_copy(zz).wait_send()

        @pl.when(zz != z)
        def _():
            z_copy(zz, z, zz).wait_send()

    each(depth, drain)


def hand_over(pieces, *refs):
    load_sem, store_sem = refs[-2:]
    moves = []
    for src, dst, held in zip(refs[:3], refs[3:6], refs[6:9]):
        count = pieces if src.shape[-2] * src.shape[-1] > 65536 * pieces else 1
        step = src.shape[-2] // count
        for i in range(count):
            cut = (0,) * (len(src.shape) - 2) + (pl.ds(i * step, step),)
            n = len(moves)
            moves.append((
                pltpu.make_async_copy(src.at[cut], held.at[cut], load_sem.at[n]),
                pltpu.make_async_copy(held.at[cut], dst.at[cut], store_sem.at[n]),
            ))
    for load, _ in moves:
        load.start()
    for load, store in moves:
        load.wait()
        store.start()
    for _, store in moves:
        store.wait()


def local(heads, replicas, queries, keys, values, out_weight, cotangent, on_time):
    _, tokens, features = queries.shape
    value_features = values.shape[2]
    rows = out_weight.shape[0]
    model = cotangent.shape[2]
    depth = replicas // 4
    summed = (value_features + FLAG_ROWS, rows)
    hbm = pl.BlockSpec(memory_space=pltpu.HBM)
    vmem = pl.BlockSpec(memory_space=pltpu.VMEM)
    dma = pltpu.SemaphoreType.DMA
    outputs = pl.pallas_call(
        functools.partial(kernel, heads, replicas),
        out_shape=(
            jax.ShapeDtypeStruct(cotangent.shape, BF16),
            jax.ShapeDtypeStruct(values.shape, BF16),
            jax.ShapeDtypeStruct(out_weight.shape, F32),
        ),
        in_specs=[hbm] * 5 + [pl.BlockSpec(memory_space=pltpu.SMEM)],
        out_specs=(hbm, vmem, vmem),
        scratch_shapes=[
            pltpu.VMEM((tokens, features), BF16),
            pltpu.VMEM((tokens, features), BF16),
            pltpu.VMEM((tokens, value_features), BF16),
            pltpu.VMEM((tokens, model), BF16),
            pltpu.VMEM((tokens, model), BF16),
            pltpu.VMEM((heads, model, value_features), BF16),
            pltpu.VMEM((heads, tokens, value_features), BF16),
            pltpu.VMEM((tokens, value_features), F32),
            pltpu.VMEM((depth * 2, value_features, rows), F32),
            pltpu.VMEM(summed, F32),
            pltpu.VMEM((tokens, tokens), BF16),
            pltpu.VMEM((depth * 2,) + summed, BF16),
            pltpu.VMEM((depth * 2,) + summed, BF16),
            pltpu.VMEM((depth,) + summed, BF16),
            pltpu.VMEM((depth,) + summed, BF16),
            pltpu.VMEM((depth,) + summed, BF16),
            pltpu.VMEM((depth,) + summed, BF16),
            dma((5,)),
            dma((depth,)),
            dma((heads, replicas)),
            dma((replicas,)),
            dma((replicas,)),
            dma((heads, replicas)),
            dma((replicas,)),
            dma((heads, replicas)),
            dma((heads, replicas)),
            dma((heads,)),
            dma((heads,)),
            dma((depth * 2,)),
            dma((depth * 2,)),
            dma((depth,)),
            dma((depth,)),
            dma((depth,)),
            dma((depth,)),
        ],
        compiler_params=pltpu.CompilerParams(
            collective_id=0, has_side_effects=True, vmem_limit_bytes=56 * 1024 * 1024
        ),
    )(queries, keys, values, out_weight, cotangent, on_time)
    return pl.pallas_call(
        functools.partial(hand_over, 8),
        out_shape=tuple(jax.ShapeDtypeStruct(o.shape, o.dtype) for o in outputs),
        in_specs=[hbm] * 3,
        out_specs=(hbm,) * 3,
        scratch_shapes=[pltpu.VMEM(o.shape, o.dtype) for o in outputs] + [dma((10,)), dma((10,))],
        compiler_params=pltpu.CompilerParams(vmem_limit_bytes=56 * 1024 * 1024),
    )(*outputs)


def solution(mesh):
    return jax.shard_map(
        functools.partial(local, mesh.shape["head"], mesh.shape["replica"]),
        mesh=mesh,
        in_specs=(
            P("replica", None, "head"),
            P("replica", None, "head"),
            P("replica", None, "head"),
            P("replica", "head"),
            P("replica", None, None),
            P("replica"),
        ),
        out_specs=(P("replica", None, None), P("replica", None, "head"), P("replica", "head")),
        check_vma=False,
    )
```

```python
import functools
import math

import jax
import jax.numpy as jnp
from jax import lax
from jax.experimental import pallas as pl
from jax.experimental.pallas import tpu as pltpu
from jax.sharding import PartitionSpec as P

MESH = pl.DeviceIdType.MESH
FLAG_ROWS = 16
F32 = jnp.float32
BF16 = jnp.bfloat16


def dot(a, b, dims):
    return lax.dot_general(a, b, ((dims[:1], dims[1:]), ((), ())), preferred_element_type=F32)


def each(count, body):
    if count <= 4:
        for i in range(count):
            body(i)
    else:
        lax.fori_loop(0, count, lambda i, c: (body(i), c)[1], 0)


def when(cond, body):
    if isinstance(cond, bool):
        if cond:
            body()
    else:
        pl.when(cond)(body)


def kernel(
    heads, replicas,
    q_hbm, k_hbm, v_hbm, w_hbm, cot_hbm, on_ref,
    layer_hbm, value_grad_ref, weight_grad_ref,
    q, k, v, cot, layer, w_all, mixed_all, mixed_grad, part, total, weights_ref,
    core_out, core_in, x_out, x_in, z_out, z_in,
    load_sem, layer_sem,
    w_recv, up_send, down_send, partner_send, x_send, head_send, core_send,
    mixed_send, mixed_recv,
    core_out_sem, core_in_sem, x_out_sem, x_in_sem, z_out_sem, z_in_sem,
):
    depth = replicas // 4
    rows = w_hbm.shape[0]
    group = 4 * rows
    tokens = q.shape[0]
    head = lax.axis_index("head")
    me = lax.axis_index("replica")
    z, x, c = me // 4, (me // 2) % 2, me % 2

    def rep(zz, xx, cc):
        return zz * 4 + xx * 2 + cc

    sibling = (head, rep(z, x, 1 - c))
    across = (head, rep(z, 1 - x, c))

    def line(zz):
        return (head, rep(zz, x, c))

    def peer(j):
        return lax.rem(head + 1 + j, heads)

    barrier = pltpu.get_barrier_semaphore()

    def greet(device):
        pl.semaphore_signal(barrier, inc=1, device_id=device, device_id_type=MESH)

    greet(sibling)
    greet(across)
    each(heads - 1, lambda j: greet((peer(j), me)))
    each(depth, lambda zz: pl.when(zz != z)(lambda: greet(line(zz))))

    loads = [
        pltpu.make_async_copy(src, dst, load_sem.at[i])
        for i, (src, dst) in enumerate(
            ((q_hbm.at[0], q), (k_hbm.at[0], k), (v_hbm.at[0], v), (cot_hbm.at[0], cot),
             (w_hbm, w_all.at[head, pl.ds(pl.multiple_of(me * rows, rows), rows)]))
        )
    ]
    for load in [loads[4]] + loads[:4]:
        load.start()
    pl.semaphore_wait(barrier, heads + depth)

    def block(hh, rr):
        return w_all.at[hh, pl.ds(pl.multiple_of(rr * rows, rows), rows)]

    def w_copy(hh, rr, sem, device):
        return pltpu.make_async_remote_copy(
            src_ref=block(hh, rr),
            dst_ref=block(hh, rr),
            send_sem=sem,
            recv_sem=w_recv.at[hh, rr],
            device_id=device,
            device_id_type=MESH,
        )

    def w_wait(hh, rr):
        w_copy(hh, rr, core_send.at[hh, rr], sibling).wait_recv()

    def to_above(rr):
        return w_copy(head, rr, up_send.at[rr], line(z + 1))

    def to_below(rr):
        return w_copy(head, rr, down_send.at[rr], line(z - 1))

    def to_partner(hh, rr):
        return w_copy(hh, rr, partner_send.at[hh, rr], line(z + 1 - 2 * (z % 2)))

    def to_across(rr):
        return w_copy(head, rr, x_send.at[rr], across)

    def to_peer(j, rr):
        return w_copy(head, rr, head_send.at[j, rr], (peer(j), me))

    def to_core(hh, rr):
        return w_copy(hh, rr, core_send.at[hh, rr], sibling)

    def to_peers(rr):
        each(heads - 1, lambda j: to_peer(j, rr).start())

    def around(d, body):
        if isinstance(d, int) and d == 0:
            body(z)
        else:
            pl.when(z - d >= 0)(lambda: body(z - d))
            pl.when(z + d < depth)(lambda: body(z + d))

    loads[4].wait()
    pl.when(z < depth - 1)(lambda: to_above(me).start())
    pl.when(z > 0)(lambda: to_below(me).start())
    to_peers(me)
    to_across(me).start()
    to_core(head, me).start()

    def gather_z(d):
        def body(zz):
            rr = rep(zz, x, c)
            w_wait(head, rr)
            pl.when((zz < z) & (z < depth - 1))(lambda: to_above(rr).start())
            pl.when((zz > z) & (z > 0))(lambda: to_below(rr).start())
            if d % 2 == 0:
                to_peers(rr)
            to_across(rr).start()
            to_core(head, rr).start()

        around(d, body)

    def gather_x(d):
        def body(zz):
            rr = rep(zz, 1 - x, c)
            w_wait(head, rr)
            to_peers(rr)
            to_core(head, rr).start()

        around(d, body)

    def gather_y(d):
        def body(zz):
            def from_peer(j):
                rr = rep(zz, x, c)
                w_wait(peer(j), rr)
                to_partner(peer(j), rr).start()
                to_core(peer(j), rr).start()

            each(heads - 1, from_peer)

        around(d, body)

    def gather_heads(d):
        def body(zz):
            def from_peer(j):
                for xx in (x, 1 - x) if d % 2 else (1 - x,):
                    w_wait(peer(j), rep(zz, xx, c))
                    to_core(peer(j), rep(zz, xx, c)).start()

            each(heads - 1, from_peer)

        around(d, body)

    def core_wait(hh, zz):
        for xx in (0, 1):
            w_wait(hh, rep(zz, xx, 1 - c))

    for load in loads[:3]:
        load.wait()
    row = lax.broadcasted_iota(jnp.int32, (tokens, tokens), 0)
    col = lax.broadcasted_iota(jnp.int32, (tokens, tokens), 1)
    offset = (row - col).astype(F32)
    log_gamma = jnp.float32(math.log(1.0 - 2.0 ** -5.0))
    for i in range(1, heads):
        log_gamma = jnp.where(head == i, jnp.float32(math.log(1.0 - 2.0 ** (-5.0 - i))), log_gamma)
    decay = jnp.where(offset >= 0.0, jnp.exp(jnp.maximum(offset, 0.0) * log_gamma), 0.0)
    scores = dot(q[...], k[...], (1, 1)) * decay
    denom = jnp.maximum(jnp.sum(jnp.abs(scores), axis=-1, keepdims=True), 1.0)
    weights_ref[...] = (scores / denom).astype(BF16)
    mixed_all[head] = dot(weights_ref[...], v[...], (1, 0)).astype(BF16)

    def mixed_copy(j):
        return pltpu.make_async_remote_copy(
            src_ref=mixed_all.at[head],
            dst_ref=mixed_all.at[head],
            send_sem=mixed_send.at[j],
            recv_sem=mixed_recv.at[head],
            device_id=(peer(j), me),
            device_id_type=MESH,
        )

    def mixed_wait(j):
        pltpu.make_async_remote_copy(
            src_ref=mixed_all.at[peer(j)],
            dst_ref=mixed_all.at[peer(j)],
            send_sem=mixed_send.at[j],
            recv_sem=mixed_recv.at[peer(j)],
            device_id=(peer(j), me),
            device_id_type=MESH,
        ).wait_recv()

    each(heads - 1, lambda j: mixed_copy(j).start())

    on = on_ref[0].astype(F32)
    features = part.shape[1]
    flags = jnp.full((FLAG_ROWS, rows), 1.0, F32) * on
    body_rows = pl.ds(0, features)
    flag_rows = pl.ds(features, FLAG_ROWS)

    def order(i):
        if isinstance(i, int):
            return i // 2 if i % 2 == 0 else depth - 1 - i // 2
        return jnp.where(i % 2 == 0, i // 2, depth - 1 - i // 2)

    def core_copy(slot):
        return pltpu.make_async_remote_copy(
            core_out.at[slot], core_in.at[slot], core_out_sem.at[slot], core_in_sem.at[slot],
            device_id=sibling, device_id_type=MESH,
        )

    def x_copy(zz):
        return pltpu.make_async_remote_copy(
            x_out.at[zz], x_in.at[zz], x_out_sem.at[zz], x_in_sem.at[zz],
            device_id=across, device_id_type=MESH,
        )

    def z_copy(zz, source, other):
        return pltpu.make_async_remote_copy(
            z_out.at[zz], z_in.at[source], z_out_sem.at[zz], z_in_sem.at[source],
            device_id=line(other), device_id_type=MESH,
        )

    loads[3].wait()
    masked_t = dot(v[...], weights_ref[...], (0, 1)).astype(BF16) * on.astype(BF16)

    def sum_start(i):
        zz = order(i)
        at = pl.multiple_of(zz * group, group)
        product = dot(masked_t, cot[:, pl.ds(at, group)], (1, 0))
        for xx in (0, 1):
            slot = zz * 2 + xx
            first = product[:, 2 * xx * rows:(2 * xx + 1) * rows]
            second = product[:, (2 * xx + 1) * rows:(2 * xx + 2) * rows]
            part[slot] = jnp.where(c == 0, first, second)
            core_out[slot, body_rows] = jnp.where(c == 0, second, first).astype(BF16)
            core_out[slot, flag_rows] = flags.astype(BF16)
            core_copy(slot).start()

    def sum_x(i):
        zz = order(i)
        slot = zz * 2 + 1 - x
        core_copy(slot).wait_recv()
        x_out[zz, body_rows] = (
            part[slot] + core_in[slot, body_rows].astype(F32)
        ).astype(BF16)
        x_out[zz, flag_rows] = (flags + core_in[slot, flag_rows].astype(F32)).astype(BF16)
        x_copy(zz).start()

    def local_sum(zz):
        slot = zz * 2 + x
        core_copy(slot).wait_recv()
        x_copy(zz).wait_recv()
        main = (
            part[slot]
            + core_in[slot, body_rows].astype(F32)
            + x_in[zz, body_rows].astype(F32)
        )
        flag = (
            flags + core_in[slot, flag_rows].astype(F32) + x_in[zz, flag_rows].astype(F32)
        )
        return main, flag

    def sum_z(i):
        zz = order(i)

        @pl.when(zz != z)
        def _():
            main, flag = local_sum(zz)
            z_out[zz, body_rows] = main.astype(BF16)
            z_out[zz, flag_rows] = flag.astype(BF16)
            z_copy(zz, z, zz).start()

    def sum_end():
        main, flag = local_sum(z)
        total[body_rows] = main
        total[flag_rows] = flag

        def add(source):
            @pl.when(source != z)
            def _():
                z_copy(z, source, source).wait_recv()
                total[...] += z_in[source].astype(F32)

        each(depth, add)
        weight_grad_ref[...] = (total[body_rows] / total[pl.ds(features, 1)]).T

    def columns(zz):
        return pl.ds(pl.multiple_of(zz * group, group), group)

    def grad_group(d):
        def body(zz):
            core_wait(head, zz)
            mixed_grad[...] += dot(cot[:, columns(zz)], w_all[head, columns(zz)], (1, 0))

        around(d, body)

    def layer_copy(zz):
        return pltpu.make_async_copy(
            layer.at[:, columns(zz)], layer_hbm.at[0, :, columns(zz)], layer_sem.at[zz]
        )

    def term(hh, zz):
        return dot(mixed_all[hh], w_all[hh, columns(zz)], (1, 1)).astype(BF16).astype(F32)

    def layer_group(d):
        def body(zz):
            each(heads - 1, lambda j: core_wait(peer(j), zz))
            total = term(0, zz)
            if heads <= 4:
                for i in range(1, heads):
                    total = total + term(i, zz)
            else:
                total = lax.fori_loop(1, heads, lambda i, t: t + term(i, zz), total)
            layer[:, columns(zz)] = total.astype(BF16)
            layer_copy(zz).start()

        around(d, body)

    gather_z(1)
    for i in range(depth):
        sum_start(i)
        if i == 0:
            gather_x(0)
            gather_y(0)
        if i > 0:
            sum_x(i - 1)
    sum_x(depth - 1)
    mixed_grad[...] = jnp.zeros_like(mixed_grad)
    for d in range(2, depth):
        gather_z(d)
        sum_z(d - 2)
        gather_x(d - 1)
        if d % 2:
            gather_y(d - 1)
    sum_z(depth - 2)
    sum_z(depth - 1)
    each(heads - 1, mixed_wait)
    for i in range(depth):
        gather_heads(i)
        grad_group(i)
        if i == 0:
            gather_x(depth - 1)
        if i < depth - 1:
            layer_group(i)
    value_grad_ref[0] = dot(
        weights_ref[...], mixed_grad[...].astype(BF16), (0, 0)
    ).astype(BF16)
    sum_end()
    layer_group(depth - 1)

    each(depth, lambda i: layer_copy(i).wait())
    each(heads - 1, lambda j: mixed_copy(j).wait_send())

    def drain(zz):
        rr = rep(zz, x, c)
        far = rep(zz, 1 - x, c)

        def one(hh):
            to_core(hh, rr).wait_send()
            to_core(hh, far).wait_send()

        each(heads, one)
        each(heads - 1, lambda j: to_peer(j, far).wait_send())

        @pl.when((zz + z) % 2 == 0)
        def _():
            def shared(j):
                to_peer(j, rr).wait_send()
                to_partner(peer(j), rr).wait_send()

            each(heads - 1, shared)

        pl.when((zz <= z) & (z < depth - 1))(lambda: to_above(rr).wait_send())
        pl.when((zz >= z) & (z > 0))(lambda: to_below(rr).wait_send())
        to_across(rr).wait_send()
        core_copy(zz * 2).wait_send()
        core_copy(zz * 2 + 1).wait_send()
        x_copy(zz).wait_send()

        @pl.when(zz != z)
        def _():
            z_copy(zz, z, zz).wait_send()

    each(depth, drain)


def hand_over(pieces, *refs):
    load_sem, store_sem = refs[-2:]
    moves = []
    for src, dst, held in zip(refs[:3], refs[3:6], refs[6:9]):
        count = pieces if src.shape[-2] * src.shape[-1] > 65536 * pieces else 1
        step = src.shape[-2] // count
        for i in range(count):
            cut = (0,) * (len(src.shape) - 2) + (pl.ds(i * step, step),)
            n = len(moves)
            moves.append((
                pltpu.make_async_copy(src.at[cut], held.at[cut], load_sem.at[n]),
                pltpu.make_async_copy(held.at[cut], dst.at[cut], store_sem.at[n]),
            ))
    for load, _ in moves:
        load.start()
    for load, store in moves:
        load.wait()
        store.start()
    for _, store in moves:
        store.wait()


def local(heads, replicas, queries, keys, values, out_weight, cotangent, on_time):
    _, tokens, features = queries.shape
    value_features = values.shape[2]
    rows = out_weight.shape[0]
    model = cotangent.shape[2]
    depth = replicas // 4
    summed = (value_features + FLAG_ROWS, rows)
    hbm = pl.BlockSpec(memory_space=pltpu.HBM)
    vmem = pl.BlockSpec(memory_space=pltpu.VMEM)
    dma = pltpu.SemaphoreType.DMA
    outputs = pl.pallas_call(
        functools.partial(kernel, heads, replicas),
        out_shape=(
            jax.ShapeDtypeStruct(cotangent.shape, BF16),
            jax.ShapeDtypeStruct(values.shape, BF16),
            jax.ShapeDtypeStruct(out_weight.shape, F32),
        ),
        in_specs=[hbm] * 5 + [pl.BlockSpec(memory_space=pltpu.SMEM)],
        out_specs=(hbm, vmem, vmem),
        scratch_shapes=[
            pltpu.VMEM((tokens, features), BF16),
            pltpu.VMEM((tokens, features), BF16),
            pltpu.VMEM((tokens, value_features), BF16),
            pltpu.VMEM((tokens, model), BF16),
            pltpu.VMEM((tokens, model), BF16),
            pltpu.VMEM((heads, model, value_features), BF16),
            pltpu.VMEM((heads, tokens, value_features), BF16),
            pltpu.VMEM((tokens, value_features), F32),
            pltpu.VMEM((depth * 2, value_features, rows), F32),
            pltpu.VMEM(summed, F32),
            pltpu.VMEM((tokens, tokens), BF16),
            pltpu.VMEM((depth * 2,) + summed, BF16),
            pltpu.VMEM((depth * 2,) + summed, BF16),
            pltpu.VMEM((depth,) + summed, BF16),
            pltpu.VMEM((depth,) + summed, BF16),
            pltpu.VMEM((depth,) + summed, BF16),
            pltpu.VMEM((depth,) + summed, BF16),
            dma((5,)),
            dma((depth,)),
            dma((heads, replicas)),
            dma((replicas,)),
            dma((replicas,)),
            dma((heads, replicas)),
            dma((replicas,)),
            dma((heads, replicas)),
            dma((heads, replicas)),
            dma((heads,)),
            dma((heads,)),
            dma((depth * 2,)),
            dma((depth * 2,)),
            dma((depth,)),
            dma((depth,)),
            dma((depth,)),
            dma((depth,)),
        ],
        compiler_params=pltpu.CompilerParams(
            collective_id=0, has_side_effects=True, vmem_limit_bytes=56 * 1024 * 1024
        ),
    )(queries, keys, values, out_weight, cotangent, on_time)
    return pl.pallas_call(
        functools.partial(hand_over, 8),
        out_shape=tuple(jax.ShapeDtypeStruct(o.shape, o.dtype) for o in outputs),
        in_specs=[hbm] * 3,
        out_specs=(hbm,) * 3,
        scratch_shapes=[pltpu.VMEM(o.shape, o.dtype) for o in outputs] + [dma((10,)), dma((10,))],
        compiler_params=pltpu.CompilerParams(vmem_limit_bytes=56 * 1024 * 1024),
    )(*outputs)


def solution(mesh):
    return jax.shard_map(
        functools.partial(local, mesh.shape["head"], mesh.shape["replica"]),
        mesh=mesh,
        in_specs=(
            P("replica", None, "head"),
            P("replica", None, "head"),
            P("replica", None, "head"),
            P("replica", "head"),
            P("replica", None, None),
            P("replica"),
        ),
        out_specs=(P("replica", None, None), P("replica", None, "head"), P("replica", "head")),
        check_vma=False,
    )
```
